256 devices in a mesh: tab: 64 (over y, z_hi, x, core), row: 4 (over z_lo).
Axes of the slice: x: 4, y: 4, z: 8 (z_hi: 2, z_lo: 4; z = z_hi * 4 + z_lo), core: 2. Of those that a mesh axis runs over, the one named last changes fastest.
Arguments:
- inputs: bfloat16 [32768, 1152], P(('tab', 'row')), may hold values from -6 to 6
- cotangent: bfloat16 [32768, 1152], P(('tab', 'row')), may hold values from -3 to 3
- cross_down: bfloat16 [1152, 512], replicated, may hold values from -0.1875 to 0.1875
- cross_up: bfloat16 [512, 1152], replicated, may hold values from -0.25 to 0.25
- cross_bias: float32 [1152], replicated, may hold values from -4 to 4
- indices: int32 [32768, 8, 8], P(('tab', 'row')), may hold values from 0 to 32767, as said below
- emb_table: float32 [262144, 128], P(('tab', 'row')), may hold values from -6 to 6
- row_accum: float32 [262144], P(('tab', 'row')), may hold values from 0.01 to 1
Outputs:
- table_new: float32 [262144, 128], P(('tab', 'row'))
- accum_new: float32 [262144], P(('tab', 'row'))
- dense_grad: bfloat16 [32768, 128], P(('tab', 'row'))
- weight_grads: float32 [1024, 1152], P(('tab', 'row'))
The draws below stay inside these ranges and needn't reach their ends.
Inputs may be any that keep to these rules, and one draw needn't show every extreme that they name: `indices`: row numbers within each table. In every aligned block of 128 samples, the 1024 lookups of each table fall exactly 32 times into each range of 1024 consecutive row numbers starting at a multiple of 1024.
All inputs are finite; a program needn't handle non-finite values.
Results may differ from the reference program's by a relative error of at most 0.0049.
Values may be sent and summed in bfloat16 or wider, within the bound.
No kernel may reach another device: no remote copies, remote signals or barrier semaphores. Data moves between devices by JAX's collectives and lax.ppermute only.
A program may use at most 64 MiB of HBM per device.

```python
import math
import jax
import jax.numpy as jnp
from jax import lax

EMB = 128
TABLES = 8
RANK = 512
HOT = 8
B_DEV = 128
ROWS_DEV = 1024
FEATURES = 1152
BATCH = 32768
ROWS_T = 32768
CAP = 32


def draw_indices(key, part):
    key = jax.random.fold_in(key, 11)
    first_key, second_key = jax.random.split(key)
    blocks = BATCH // B_DEV
    ranges = ROWS_T // ROWS_DEV
    lookups = B_DEV * HOT
    base = jnp.repeat(jnp.arange(ranges, dtype=jnp.int32), CAP)
    base = jnp.broadcast_to(base, (blocks, TABLES, lookups))
    spread = jax.random.permutation(first_key, base, axis=2, independent=True)
    offset = jax.random.randint(second_key, (blocks, TABLES, lookups), 0, ROWS_DEV, dtype=jnp.int32)
    picked = spread * ROWS_DEV + offset
    picked = picked.reshape(blocks, TABLES, B_DEV, HOT).transpose(0, 2, 1, 3)
    return picked.reshape(BATCH, TABLES, HOT)


def block_scale(stream_key, dims, cuts, low, top_value):
    def one(dim, shards_of):
        draws = jax.random.uniform(jax.random.fold_in(jax.random.fold_in(stream_key, 6), dim), (shards_of,), jnp.float32, low / len(cuts), top_value / len(cuts))
        return jnp.repeat(jnp.exp(draws), dims[dim] // shards_of).reshape((-1,) + (1,) * (len(dims) - dim - 1))

    gain = one(*cuts[0])
    for cut in cuts[1:]:
        gain = gain * one(*cut)
    return gain


def centred(key, shape, width, reach, cuts=(), kind=jnp.bfloat16):
    factor_of = block_scale(key, shape, cuts, -0.22, 0.18) if cuts else 1.0
    entries = jax.random.normal(key, shape, jnp.float32) * width * factor_of
    return jnp.minimum(jnp.maximum(entries, -reach), reach).astype(kind)


def setup_inputs(seed: int = 0) -> dict:
    splits = jax.random.split(jax.random.key(seed), 9)
    return {
        "inputs": centred(splits[0], (BATCH, FEATURES), 1.0, 6.0, ((0, 256),)),
        "cotangent": centred(splits[1], (BATCH, FEATURES), 0.2, 3.0, ((0, 256),)),
        "cross_down": centred(splits[2], (FEATURES, RANK), FEATURES ** -0.5, 0.1875),
        "cross_up": centred(splits[3], (RANK, FEATURES), RANK ** -0.5, 0.25),
        "cross_bias": centred(splits[4], (FEATURES,), 0.5, 4.0, (), jnp.float32),
        "indices": draw_indices(jax.random.fold_in(splits[8], 71), 0),
        "emb_table": centred(splits[6], (TABLES * ROWS_T, EMB), 1.0, 6.0, ((0, 256),), jnp.float32),
        "row_accum": jnp.clip(jnp.exp(math.log(1.0) - 4.6051702 * jax.random.uniform(splits[7], (TABLES * ROWS_T,), jnp.float32) ** block_scale(splits[7], (TABLES * ROWS_T,), ((0, 256),), -0.2, 0.2)), 0.01, 1.0),
    }


RATE = 0.1
EPSILON = 1e-08

def reference(inputs, cotangent, cross_down, cross_up, cross_bias, indices, emb_table, row_accum):
    blocks = BATCH // B_DEV
    shifts = (jnp.arange(TABLES, dtype=jnp.int32) * ROWS_T)[None, :, None]

    def advance(carry, item):
        weight_terms, row_grads = carry
        block_in, block_cot, block_idx = item
        hidden = jnp.dot(block_in, cross_down, preferred_element_type=jnp.float32).astype(jnp.bfloat16)
        cross_scale = jnp.dot(hidden, cross_up, preferred_element_type=jnp.float32) + cross_bias
        upward = block_cot.astype(jnp.float32)
        grad_scale = (upward * block_in.astype(jnp.float32)).astype(jnp.bfloat16)
        grad_hidden = jnp.dot(grad_scale, cross_up.T, preferred_element_type=jnp.float32).astype(jnp.bfloat16)
        grad_input = upward * (cross_scale + 1.0) + jnp.dot(grad_hidden, cross_down.T, preferred_element_type=jnp.float32)
        dense_part = grad_input[:, :EMB].astype(jnp.bfloat16)
        pooled = grad_input[:, EMB:].astype(jnp.bfloat16).reshape(B_DEV, TABLES, EMB)
        stacked = jnp.concatenate([jnp.dot(grad_hidden.T, block_in, preferred_element_type=jnp.float32), jnp.dot(hidden.T, grad_scale, preferred_element_type=jnp.float32)], axis=0)
        weight_terms = weight_terms + stacked
        flat_rows = (block_idx + shifts).reshape(-1)
        spread = jnp.broadcast_to(pooled[:, :, None, :], (B_DEV, TABLES, HOT, EMB)).reshape(-1, EMB).astype(jnp.float32)
        row_grads = row_grads.at[flat_rows].add(spread)
        return ((weight_terms, row_grads), dense_part)
    start = (jnp.zeros((2 * RANK, FEATURES), jnp.float32), jnp.zeros((TABLES * ROWS_T, EMB), jnp.float32))
    items = (inputs.reshape(blocks, B_DEV, FEATURES), cotangent.reshape(blocks, B_DEV, FEATURES), indices.reshape(blocks, B_DEV, TABLES, HOT))
    (weight_terms, row_grads), dense_parts = lax.scan(advance, start, items)
    accum_new = row_accum + lax.optimization_barrier(jnp.mean(row_grads * row_grads, axis=1))
    table_new = emb_table - RATE * row_grads / (jnp.sqrt(accum_new) + EPSILON)[:, None]
    return (table_new, accum_new, dense_parts.reshape(BATCH, EMB), weight_terms)
```

```python
import jax
import jax.numpy as jnp
from jax import lax
from jax.experimental import pallas as pl
from jax.experimental.pallas import tpu as pltpu
from jax.sharding import Mesh, PartitionSpec as P

EMB = 128
TABLES = 8
HOT = 8
RATE = 0.1
EPSILON = 1e-08
BLOCK = 128
ROWS = 1024
SLOTS = 32
META = 16
AXES = ("y", "zh", "x", "c", "zl")
NY, NZH, NX, NC, NZL = 4, 2, 4, 2, 4


def dot(a, b, dims):
    return lax.dot_general(a, b, ((dims[0], dims[1]), ((), ())), preferred_element_type=jnp.float32)


def expand_kernel(core_ref, own_ref, other_ref, out_ref, look_ref, row_ref):
    core = core_ref[0]
    lane_group = lax.broadcasted_iota(jnp.int32, (8, 128), 1) // SLOTS
    sample_iota = lax.broadcasted_iota(jnp.int32, (BLOCK, 128), 0).astype(jnp.float32)

    def gather(ref, first):
        def step(j, _):
            looks, rows = [], []
            for m in range(NX):
                b = j * NX + m
                meta = ref[b, BLOCK:BLOCK + META, :].astype(jnp.float32)
                mine = jnp.where(core == 0, meta[0:8], meta[8:16])
                pick = (sample_iota == mine[0:1]).astype(jnp.bfloat16)
                looks.append(dot(pick, ref[b, 0:BLOCK, :], ((0,), (0,))).astype(jnp.bfloat16))
                rows.append(jnp.broadcast_to(mine[1:2] * 32.0 + mine[2:3], (8, 128)))
            for d in range(NX):
                row = rows[d]
                for g in range(NX):
                    m = (d - g) % NX
                    look_ref[d, first + j, g * SLOTS:(g + 1) * SLOTS, :] = looks[m][g * SLOTS:(g + 1) * SLOTS]
                    if g:
                        row = jnp.where(lane_group == g, rows[m], row)
                row_ref[d, first + j] = row
            return 0

        lax.fori_loop(0, 8, step, 0)

    gather(own_ref, 0)
    gather(other_ref, 8)

    base = lax.broadcasted_iota(jnp.int32, (256, 128), 0).astype(jnp.float32)
    for d in range(NX):
        def rows_step(i, _, d=d):
            here = base + (i * 256).astype(jnp.float32)
            hot = jnp.concatenate(
                [(here == row_ref[d, j, 0:1, :]).astype(jnp.bfloat16) for j in range(16)], axis=1
            )
            total = dot(hot, look_ref[d].reshape(16 * 128, EMB), ((1,), (0,)))
            out_ref[d, pl.ds(pl.multiple_of(i * 256, 256), 256), :] = total.astype(jnp.bfloat16)
            return 0

        lax.fori_loop(0, ROWS // 256, rows_step, 0)


def update_kernel(a_ref, b_ref, c_ref, d_ref, table_ref, accum_ref, table_out, accum_out):
    eye = lax.broadcasted_iota(jnp.int32, (128, 128), 0) == lax.broadcasted_iota(jnp.int32, (128, 128), 1)
    for i in range(ROWS // 128):
        s = slice(i * 128, (i + 1) * 128)
        grad = a_ref[s].astype(jnp.float32) + b_ref[s].astype(jnp.float32)
        grad = grad + (c_ref[s].astype(jnp.float32) + d_ref[s].astype(jnp.float32))
        mean = jnp.sum(grad * grad, axis=1, keepdims=True) * (1.0 / EMB)
        old = jnp.sum(jnp.where(eye, accum_ref[i:i + 1, :], 0.0), axis=1, keepdims=True)
        new = old + mean
        table_out[s] = table_ref[s] - grad * (RATE / (jnp.sqrt(new) + EPSILON))
        accum_out[i:i + 1, :] = jnp.sum(jnp.where(eye, new, 0.0), axis=0, keepdims=True)


def ring(size, shift):
    return [(i, (i + shift) % size) for i in range(size)]


def per_device(inputs, cotangent, cross_down, cross_up, cross_bias, indices, emb_table, row_accum):
    x = lax.axis_index("x")
    c = lax.axis_index("c")
    zl = lax.axis_index("zl")
    swap = ring(NC, 1)

    idx = jnp.transpose(indices, (1, 0, 2)).reshape(TABLES, BLOCK * HOT)
    sample = lax.broadcasted_iota(jnp.int32, idx.shape, 1) // HOT
    owner = idx >> 10
    place = (owner & 3) * 8 + ((owner >> 2) & 1) * 4 + (((owner >> 3) - x - zl) & 3)
    keys = lax.sort((place << 17) | ((idx & 1023) << 7) | sample, dimension=1, is_stable=False)

    hidden = dot(inputs, cross_down, ((1,), (0,))).astype(jnp.bfloat16)
    upward = cotangent.astype(jnp.float32)
    grad_scale = (upward * inputs.astype(jnp.float32)).astype(jnp.bfloat16)
    grad_hidden = dot(grad_scale, cross_up, ((1,), (1,))).astype(jnp.bfloat16)
    cross_scale = dot(hidden, cross_up, ((1,), (0,))) + cross_bias
    grad_input = upward * (cross_scale + 1.0) + dot(grad_hidden, cross_down, ((1,), (1,)))
    dense_part = grad_input[:, :EMB].astype(jnp.bfloat16)
    pooled = grad_input[:, EMB:].astype(jnp.bfloat16).reshape(BLOCK, TABLES, EMB)

    keys = keys.reshape(TABLES, NZL, NC, 1, 128)
    fields = jnp.concatenate(
        [keys & 127, (keys >> 12) & 31, (keys >> 7) & 31, jnp.zeros((TABLES, NZL, NC, 5, 128), jnp.int32)], axis=3
    ).astype(jnp.bfloat16).reshape(TABLES, NZL, META, 128)
    blocks = jnp.broadcast_to(jnp.transpose(pooled, (1, 0, 2))[:, None], (TABLES, NZL, BLOCK, EMB))
    sent = jnp.concatenate([blocks, fields], axis=2).reshape(TABLES * NZL, BLOCK + META, EMB)
    own = lax.all_to_all(sent, ("y", "zh", "zl"), split_axis=0, concat_axis=0, tiled=True)
    other = lax.ppermute(own, "c", swap)

    partial = pl.pallas_call(
        expand_kernel,
        out_shape=jax.ShapeDtypeStruct((NX, ROWS, EMB), jnp.bfloat16),
        in_specs=[
            pl.BlockSpec(memory_space=pltpu.SMEM),
            pl.BlockSpec(memory_space=pltpu.VMEM),
            pl.BlockSpec(memory_space=pltpu.VMEM),
        ],
        out_specs=pl.BlockSpec(memory_space=pltpu.VMEM),
        scratch_shapes=[
            pltpu.VMEM((NX, 16, 128, EMB), jnp.bfloat16),
            pltpu.VMEM((NX, 16, 8, 128), jnp.float32),
        ],
        compiler_params=pltpu.CompilerParams(vmem_limit_bytes=32 * 1024 * 1024),
        cost_estimate=pl.CostEstimate(flops=2_500_000_000, bytes_accessed=3_500_000, transcendentals=0),
    )(c.astype(jnp.int32).reshape(1), own, other)
    arrived = [lax.ppermute(partial[d], "x", ring(NX, d)) for d in range(1, NX)]

    spread = lax.broadcasted_iota(jnp.int32, (512, 256), 0)
    column = lax.broadcasted_iota(jnp.int32, (512, 256), 1)

    def rows_of(core):
        choose = (spread == (column // 16) * 32 + core * 16 + column % 16).astype(jnp.bfloat16)
        return [dot(v, choose, ((1,), (0,))).astype(jnp.bfloat16) for v in (grad_hidden, hidden)]

    kept = rows_of(c)
    other_in = lax.ppermute(inputs, "c", swap)
    other_scale = lax.ppermute(grad_scale, "c", swap)
    other_cols = lax.ppermute(jnp.concatenate(rows_of(1 - c), axis=1), "c", swap)
    top = dot(
        jnp.concatenate([kept[0], other_cols[:, :256]], axis=0), jnp.concatenate([inputs, other_in], axis=0), ((0,), (0,))
    )
    bottom = dot(
        jnp.concatenate([kept[1], other_cols[:, 256:]], axis=0), jnp.concatenate([grad_scale, other_scale], axis=0), ((0,), (0,))
    )
    terms = jnp.concatenate([top, bottom], axis=0).astype(jnp.bfloat16).reshape(NY, 128, 1152)
    terms = lax.all_to_all(terms, "y", split_axis=0, concat_axis=0, tiled=True)
    terms = jnp.sum(terms.astype(jnp.float32), axis=0).astype(jnp.bfloat16)
    terms = jnp.transpose(terms.reshape(NZH, NX, NZL, 4, 1152), (0, 2, 1, 3, 4)).reshape(32, 4, 1152)
    terms = lax.all_to_all(terms, ("zh", "zl", "x"), split_axis=0, concat_axis=0, tiled=True)
    weight_total = jnp.sum(terms.astype(jnp.float32), axis=0)

    table_new, accum_new = pl.pallas_call(
        update_kernel,
        out_shape=(
            jax.ShapeDtypeStruct((ROWS, EMB), jnp.float32),
            jax.ShapeDtypeStruct((8, 128), jnp.float32),
        ),
        in_specs=[pl.BlockSpec(memory_space=pltpu.VMEM)] * 6,
        out_specs=(pl.BlockSpec(memory_space=pltpu.VMEM),) * 2,
        compiler_params=pltpu.CompilerParams(vmem_limit_bytes=16 * 1024 * 1024),
        cost_estimate=pl.CostEstimate(flops=2_000_000, bytes_accessed=2_100_000, transcendentals=0),
    )(partial[0], *arrived, emb_table, row_accum.reshape(8, 128))
    return (table_new, accum_new.reshape(ROWS), dense_part, weight_total)


def solution(mesh):
    fine = Mesh(mesh.devices.reshape(NY, NZH, NX, NC, NZL), AXES)
    in_specs = (
        P(AXES, None), P(AXES, None), P(), P(), P(), P(AXES, None, None), P(AXES, None), P(AXES),
    )
    out_specs = (P(AXES, None), P(AXES), P(AXES, None), P(AXES, None))
    return jax.shard_map(per_device, mesh=fine, in_specs=in_specs, out_specs=out_specs, check_vma=False)
```

```python
import functools

import jax
import jax.numpy as jnp
from jax import lax
from jax.experimental import pallas as pl
from jax.experimental.pallas import tpu as pltpu
from jax.sharding import Mesh, PartitionSpec as P

EMB = 128
TABLES = 8
HOT = 8
RANK = 512
FEATURES = 1152
RATE = 0.1
EPSILON = 1e-08
BLOCK = 128
ROWS = 1024
SLOTS = 32
META = 16
AXES = ("y", "zh", "x", "c", "zl")
NY, NZH, NX, NC, NZL = 4, 2, 4, 2, 4
PACK = 2 * FEATURES + RANK
VMEM = pl.BlockSpec(memory_space=pltpu.VMEM)
BF16, F32, I32 = jnp.bfloat16, jnp.float32, jnp.int32


def dot(a, b, left, right):
    return lax.dot_general(a, b, (((left,), (right,)), ((), ())), preferred_element_type=F32)


def iota(shape, dim):
    return lax.broadcasted_iota(I32, shape, dim)


def params(mib):
    return pltpu.CompilerParams(vmem_limit_bytes=mib * 1024 * 1024)


def cost(flops, bytes_accessed):
    return pl.CostEstimate(flops=flops, bytes_accessed=bytes_accessed, transcendentals=0)


def spot(axis):
    return lax.axis_index(axis)


def rank_kernel(idx_ref, meta_ref):
    yy, xx = spot("y"), spot("x")
    upper = (iota((128, 128), 0) < iota((128, 128), 1)).astype(BF16)
    ones = jnp.ones((128, 128), BF16)
    sub32 = iota((32, 128), 0)
    sub128 = iota((128, 128), 0)
    pair = iota((META, 128), 0) // 2
    second = iota((META, 128), 0) % 2 == 1
    for t in range(TABLES):
        ahead = (t // 2 - yy) & 3
        idx = idx_ref[t * HOT:(t + 1) * HOT, :]
        owner = idx >> 10
        place = (owner & 3) * 2 + ((owner >> 2) & 1)
        group = ((owner >> 3) - xx - ahead) & 3
        full = place * 4 + group
        high = ((idx >> 2) & 255).astype(F32)
        low = ((idx & 3) * 128 + iota((HOT, 128), 1) - 256).astype(F32)
        hot = jnp.concatenate([(sub32 == full[k:k + 1]).astype(F32) for k in range(HOT)], axis=0)
        hot16 = hot.astype(BF16)
        before = dot(hot16, upper, 1, 0)
        total = dot(hot16, ones, 1, 0)
        base = jnp.zeros((32, 128), F32)
        slots, values = [], []
        for k in range(HOT):
            s = slice(k * 32, (k + 1) * 32)
            rank = jnp.sum(hot[s] * (before[s] + base), axis=0, keepdims=True).astype(I32)
            base = base + total[s]
            slots.append((sub128 == group[k:k + 1] * SLOTS + rank).astype(F32).astype(BF16))
            value = jnp.where(second, low[k:k + 1], high[k:k + 1])
            values.append(jnp.where(pair == place[k:k + 1], value, 0.0).astype(BF16))
        meta = dot(jnp.concatenate(values, axis=1), jnp.concatenate(slots, axis=1), 1, 1)
        meta_ref[t] = meta.astype(BF16)


def hidden_kernel(in_ref, cot_ref, down_ref, up_ref, pack_ref, cols_ref, both_ref):
    yy, core = spot("y"), spot("c")
    inputs = in_ref[...]
    grad_scale = (cot_ref[...].astype(F32) * inputs.astype(F32)).astype(BF16)
    pack_ref[:, :FEATURES] = inputs
    pack_ref[:, FEATURES:2 * FEATURES] = grad_scale
    hidden = dot(inputs, down_ref[...], 1, 0).astype(BF16)
    grad_hidden = dot(grad_scale, up_ref[...], 1, 1).astype(BF16)
    both_ref[:, :RANK] = grad_hidden
    both_ref[:, RANK:] = hidden

    both = jnp.concatenate([grad_hidden, hidden], axis=1)
    src = iota((2 * RANK, RANK), 0)
    dst = iota((2 * RANK, RANK), 1)
    from_y = ((dst >> 7) + yy) & 3
    want = from_y * 256 + ((dst >> 6) & 1) * 128 + ((dst >> 2) & 3) * 32 + ((dst >> 4) & 3) * 4 + (dst & 3)
    pack_ref[:, 2 * FEATURES:] = dot(both, (src == want + (1 - core) * 16).astype(F32).astype(BF16), 1, 0).astype(BF16)
    cols_ref[...] = dot(both, (src == want + core * 16).astype(F32).astype(BF16), 1, 0).astype(BF16)


def pooled_kernel(cot_ref, both_ref, down_ref, up_ref, bias_ref, meta_ref, dense_ref, sent_ref):
    yy, half = spot("y"), spot("zh")
    bias = jnp.concatenate([bias_ref[i:i + 1, :] for i in range(FEATURES // 128)], axis=1)
    scale = dot(both_ref[:, RANK:], up_ref[...], 1, 0) + bias
    back = dot(both_ref[:, :RANK], down_ref[...], 1, 1)
    grad = (cot_ref[...].astype(F32) * (scale + 1.0) + back).astype(BF16)
    dense_ref[...] = grad[:, :EMB]
    for t in range(TABLES):
        ahead, other = (t // 2 - yy) & 3, (t % 2) ^ half
        sent_ref[ahead, other, 0:BLOCK, :] = grad[:, (t + 1) * EMB:(t + 2) * EMB]
        sent_ref[ahead, other, BLOCK:BLOCK + META, :] = meta_ref[t]


def weight_kernel(pack_ref, cols_ref, other_ref, out_ref):
    yy = spot("y")
    for d in range(NY):
        to = (yy + d) & 3
        s = slice(d * 128, (d + 1) * 128)
        left = jnp.concatenate([cols_ref[:, s], other_ref[:, 2 * FEATURES + d * 128:2 * FEATURES + (d + 1) * 128]], axis=0)

        def put(first):
            right = jnp.concatenate([pack_ref[:, first:first + FEATURES], other_ref[:, first:first + FEATURES]], axis=0)
            out_ref[to] = dot(left, right, 0, 0).astype(BF16)

        pl.when(to < 2)(functools.partial(put, 0))
        pl.when(to >= 2)(functools.partial(put, FEATURES))


def add_kernel(in_ref, out_ref):
    total = in_ref[0].astype(F32)
    for i in range(1, in_ref.shape[0]):
        total = total + in_ref[i].astype(F32)
    if len(out_ref.shape) == 2:
        out_ref[...] = total.astype(out_ref.dtype)
    else:
        size = out_ref.shape[1]
        for i in range(out_ref.shape[0]):
            out_ref[i] = total[i * size:(i + 1) * size].astype(out_ref.dtype)


def expand(place, refs, look_ref, row_ref):
    lane_group = iota((8, 128), 1) // SLOTS
    sample_iota = iota((BLOCK, 128), 0)
    meta_row = iota((META, 128), 0)
    for j, ref in enumerate(refs):
        looks, rows = [], []
        for m in range(NY):
            b = m * (BLOCK + META)
            meta = ref[b + BLOCK:b + BLOCK + META, :].astype(F32)
            high = jnp.sum(jnp.where(meta_row == place * 2, meta, 0.0), axis=0, keepdims=True).astype(I32)
            low = jnp.sum(jnp.where(meta_row == place * 2 + 1, meta, 0.0), axis=0, keepdims=True).astype(I32) + 256
            pick = (sample_iota == (low & 127)).astype(F32).astype(BF16)
            looks.append(dot(pick, ref[b:b + BLOCK, :], 0, 0).astype(BF16))
            rows.append(jnp.broadcast_to((high * 4 + (low >> 7)).astype(F32), (8, 128)))
        for d in range(NX):
            row = rows[d]
            for g in range(NX):
                m = (d - g) % NX
                look_ref[d, j, g * SLOTS:(g + 1) * SLOTS, :] = looks[m][g * SLOTS:(g + 1) * SLOTS]
                if g:
                    row = jnp.where(lane_group == g, rows[m], row)
            row_ref[d, j] = row


def scatter(d, looks, rows, out_ref, first=None):
    base = iota((256, 128), 0).astype(F32)
    look = jnp.concatenate([ref[d].reshape(-1, EMB) for ref in looks], axis=0)
    for i in range(ROWS // 256):
        here = base + float(i * 256)
        s = slice(i * 256, (i + 1) * 256)
        hot = jnp.concatenate([(here == ref[d, j, 0:1, :]).astype(BF16) for ref in rows for j in range(ref.shape[1])], axis=1)
        total = dot(hot, look, 1, 0)
        if first is not None:
            total = total + first[s].astype(F32)
        out_ref[s] = total.astype(BF16)


def expand_kernel(count, *refs):
    place = spot("zl") * 2 + spot("c")
    look_own, row_own, look_other, row_other = refs[count:]
    expand(place ^ 1, refs[:count], look_other, row_other)
    expand(place, refs[:count], look_own, row_own)


def scatter_kernel(ds, parts, *refs):
    looks, rows, rest = refs[:parts], refs[parts:2 * parts], refs[2 * parts:]
    count = len(ds)
    firsts, outs = rest[:-count], rest[-count:]
    for i, d in enumerate(ds):
        scatter(d, looks, rows, outs[i], firsts[i] if firsts else None)


def update_kernel(a_ref, b_ref, c_ref, d_ref, table_ref, accum_ref, table_out, accum_out):
    eye = iota((128, 128), 0) == iota((128, 128), 1)
    for i in range(ROWS // 128):
        s = slice(i * 128, (i + 1) * 128)
        grad = a_ref[s].astype(F32) + b_ref[s].astype(F32)
        grad = grad + (c_ref[s].astype(F32) + d_ref[s].astype(F32))
        mean = jnp.sum(grad * grad, axis=1, keepdims=True) * (1.0 / EMB)
        old = jnp.sum(jnp.where(eye, accum_ref[i:i + 1, :], 0.0), axis=1, keepdims=True)
        new = old + mean
        table_out[s] = table_ref[s] - grad * (RATE / (jnp.sqrt(new) + EPSILON))
        accum_out[i:i + 1, :] = jnp.sum(jnp.where(eye, new, 0.0), axis=0, keepdims=True)


def ring(size, shift):
    return [(i, (i + shift) % size) for i in range(size)]


def shape(dims, kind):
    return jax.ShapeDtypeStruct(dims, kind)


def per_device(inputs, cotangent, cross_down, cross_up, cross_bias, indices, emb_table, row_accum):
    swap = ring(NC, 1)
    idx = jnp.transpose(indices, (1, 2, 0)).reshape(TABLES * HOT, BLOCK)

    def call(kernel, name, outs, operands, mib, work):
        return pl.pallas_call(
            kernel,
            out_shape=outs,
            in_specs=[VMEM] * len(operands),
            out_specs=(VMEM,) * len(outs) if isinstance(outs, tuple) else VMEM,
            compiler_params=params(mib),
            cost_estimate=work,
            name=name,
        )(*operands)

    meta = call(rank_kernel, "rank", shape((TABLES, META, 128), BF16), (idx,), 16, cost(2_000_000_000, 100_000))
    pack, cols, both = call(
        hidden_kernel, "hidden",
        (shape((BLOCK, PACK), BF16), shape((BLOCK, RANK), BF16), shape((BLOCK, 2 * RANK), BF16)),
        (inputs, cotangent, cross_down, cross_up), 16, cost(500_000_000, 4_000_000),
    )
    dense_part, sent = call(
        pooled_kernel, "pooled",
        (shape((BLOCK, EMB), BF16), shape((NY, NZH, BLOCK + META, EMB), BF16)),
        (cotangent, both, cross_down, cross_up, cross_bias.reshape(FEATURES // 128, 128), meta),
        16, cost(300_000_000, 4_000_000),
    )

    other_pack = lax.ppermute(pack, "c", swap)
    along = [sent[0]] + [lax.ppermute(sent[d], "y", ring(NY, d)) for d in range(1, NY)]
    terms = call(
        weight_kernel, "weights", shape((NY, 128, FEATURES), BF16), (pack, cols, other_pack), 16, cost(300_000_000, 3_000_000)
    )
    along, terms = lax.optimization_barrier((along, terms))
    near = jnp.concatenate([v[0] for v in along], axis=0)
    far = jnp.concatenate([v[1] for v in along], axis=0)

    def cross(m):
        return lax.ppermute(far, ("zh", "zl"), [(i, (7 - i) ^ m) for i in range(8)])

    def line(m):
        return lax.ppermute(near, "zl", [(i, i ^ m) for i in range(NZL)])

    blocks = [near, cross(3), line(3), cross(2), line(2), cross(0), cross(1), line(1)]

    def reduced(v, axes, dims, kind):
        v = lax.all_to_all(v, axes, split_axis=0, concat_axis=0, tiled=True)
        return call(add_kernel, "add", shape(dims, kind), (v,), 16, cost(1_000_000, 1_500_000))

    def expanded(blocks):
        look = shape((NX, len(blocks), 128, EMB), BF16)
        row = shape((NX, len(blocks), 8, 128), F32)
        return call(
            functools.partial(expand_kernel, len(blocks)), "expand", (look, row, look, row), tuple(blocks), 16, cost(200_000_000, 2_400_000)
        )

    terms = reduced(terms, "y", (32, 4, FEATURES), BF16)
    lists = [expanded(blocks[:3]), expanded(blocks[3:6])]
    late, terms = lax.optimization_barrier((blocks[6:], terms))
    lists.append(expanded(late))
    own, other = [[v[i] for v in lists] + [v[i + 1] for v in lists] for i in (0, 2)]

    def scattered(arrays, ds, firsts=()):
        return call(
            functools.partial(scatter_kernel, ds, len(lists)), "scatter",
            (shape((ROWS, EMB), BF16),) * len(ds), (*arrays, *firsts), 24, cost(300_000_000 * len(ds), 2_000_000),
        )

    def swapped(vs):
        return [lax.ppermute(v, "c", swap) for v in vs]

    first = scattered(other, (2,))
    other, first = lax.optimization_barrier((other, first))
    (first,) = swapped(first)
    second = scattered(other, (1, 3))
    other, second = lax.optimization_barrier((other, second))
    second = swapped(second)
    last = scattered(other, (0,))
    own, last = lax.optimization_barrier((own, last))
    (last,) = swapped(last)
    apart = scattered(own, (2,), (first,))
    own, apart = lax.optimization_barrier((own, apart))
    apart = lax.ppermute(apart[0], "x", ring(NX, 2))
    right, left = scattered(own, (1, 3), second)
    own, right, left = lax.optimization_barrier((own, right, left))
    right = lax.ppermute(right, "x", ring(NX, 1))
    left = lax.ppermute(left, "x", ring(NX, 3))
    (here,) = scattered(own, (0,), (last,))
    here, terms = lax.optimization_barrier((here, terms))
    weight_total = reduced(terms, ("zh", "zl", "x"), (4, FEATURES), F32)

    table_new, accum_new = call(
        update_kernel, "update", (shape((ROWS, EMB), F32), shape((8, 128), F32)),
        (here, right, left, apart, emb_table, row_accum.reshape(8, 128)), 16, cost(30_000_000_000, 2_100_000),
    )
    return (table_new, accum_new.reshape(ROWS), dense_part, weight_total)


def solution(mesh):
    fine = Mesh(mesh.devices.reshape(NY, NZH, NX, NC, NZL), AXES)
    in_specs = (
        P(AXES, None), P(AXES, None), P(), P(), P(), P(AXES, None, None), P(AXES, None), P(AXES),
    )
    out_specs = (P(AXES, None), P(AXES), P(AXES, None), P(AXES, None))
    return jax.shard_map(per_device, mesh=fine, in_specs=in_specs, out_specs=out_specs, check_vma=False)
```

```python
import functools

import jax
import jax.numpy as jnp
from jax import lax
from jax.experimental import pallas as pl
from jax.experimental.pallas import tpu as pltpu
from jax.sharding import Mesh, PartitionSpec as P

EMB = 128
TABLES = 8
HOT = 8
RANK = 512
FEATURES = 1152
RATE = 0.1
EPSILON = 1e-08
BLOCK = 128
ROWS = 1024
SLOTS = 32
META = 16
AXES = ("y", "zh", "x", "c", "zl")
NY, NZH, NX, NC, NZL = 4, 2, 4, 2, 4
PACK = 2 * FEATURES + RANK
VMEM = pl.BlockSpec(memory_space=pltpu.VMEM)
BF16, F32, I32 = jnp.bfloat16, jnp.float32, jnp.int32


def dot(a, b, left, right):
    return lax.dot_general(a, b, (((left,), (right,)), ((), ())), preferred_element_type=F32)


def iota(shape, dim):
    return lax.broadcasted_iota(I32, shape, dim)


def params(mib):
    return pltpu.CompilerParams(vmem_limit_bytes=mib * 1024 * 1024)


def cost(flops, bytes_accessed):
    return pl.CostEstimate(flops=flops, bytes_accessed=bytes_accessed, transcendentals=0)


def spot(axis):
    return lax.axis_index(axis)


def rank_kernel(idx_ref, meta_ref):
    yy, xx = spot("y"), spot("x")
    upper = (iota((128, 128), 0) < iota((128, 128), 1)).astype(BF16)
    ones = jnp.ones((128, 128), BF16)
    sub32 = iota((32, 128), 0)
    sub128 = iota((128, 128), 0)
    pair = iota((META, 128), 0) // 2
    second = iota((META, 128), 0) % 2 == 1
    for t in range(TABLES):
        ahead = (t // 2 - yy) & 3
        idx = idx_ref[t * HOT:(t + 1) * HOT, :]
        owner = idx >> 10
        place = (owner & 3) * 2 + ((owner >> 2) & 1)
        group = ((owner >> 3) - xx - ahead) & 3
        full = place * 4 + group
        high = ((idx >> 2) & 255).astype(F32)
        low = ((idx & 3) * 128 + iota((HOT, 128), 1) - 256).astype(F32)
        hot = jnp.concatenate([(sub32 == full[k:k + 1]).astype(F32) for k in range(HOT)], axis=0)
        hot16 = hot.astype(BF16)
        before = dot(hot16, upper, 1, 0)
        total = dot(hot16, ones, 1, 0)
        base = jnp.zeros((32, 128), F32)
        slots, values = [], []
        for k in range(HOT):
            s = slice(k * 32, (k + 1) * 32)
            rank = jnp.sum(hot[s] * (before[s] + base), axis=0, keepdims=True).astype(I32)
            base = base + total[s]
            slots.append((sub128 == group[k:k + 1] * SLOTS + rank).astype(F32).astype(BF16))
            value = jnp.where(second, low[k:k + 1], high[k:k + 1])
            values.append(jnp.where(pair == place[k:k + 1], value, 0.0).astype(BF16))
        meta = dot(jnp.concatenate(values, axis=1), jnp.concatenate(slots, axis=1), 1, 1)
        meta_ref[t] = meta.astype(BF16)


def hidden_kernel(in_ref, cot_ref, down_ref, up_ref, pack_ref, cols_ref, both_ref):
    yy, core = spot("y"), spot("c")
    inputs = in_ref[...]
    grad_scale = (cot_ref[...].astype(F32) * inputs.astype(F32)).astype(BF16)
    pack_ref[:, :FEATURES] = inputs
    pack_ref[:, FEATURES:2 * FEATURES] = grad_scale
    hidden = dot(inputs, down_ref[...], 1, 0).astype(BF16)
    grad_hidden = dot(grad_scale, up_ref[...], 1, 1).astype(BF16)
    both_ref[:, :RANK] = grad_hidden
    both_ref[:, RANK:] = hidden

    both = jnp.concatenate([grad_hidden, hidden], axis=1)
    src = iota((2 * RANK, RANK), 0)
    dst = iota((2 * RANK, RANK), 1)
    from_y = ((dst >> 7) + yy) & 3
    want = from_y * 256 + ((dst >> 6) & 1) * 128 + ((dst >> 2) & 3) * 32 + ((dst >> 4) & 3) * 4 + (dst & 3)
    pack_ref[:, 2 * FEATURES:] = dot(both, (src == want + (1 - core) * 16).astype(F32).astype(BF16), 1, 0).astype(BF16)
    cols_ref[...] = dot(both, (src == want + core * 16).astype(F32).astype(BF16), 1, 0).astype(BF16)


def pooled_kernel(cot_ref, both_ref, down_ref, up_ref, bias_ref, meta_ref, dense_ref, sent_ref):
    yy, half = spot("y"), spot("zh")
    bias = jnp.concatenate([bias_ref[i:i + 1, :] for i in range(FEATURES // 128)], axis=1)
    scale = dot(both_ref[:, RANK:], up_ref[...], 1, 0) + bias
    back = dot(both_ref[:, :RANK], down_ref[...], 1, 1)
    grad = (cot_ref[...].astype(F32) * (scale + 1.0) + back).astype(BF16)
    dense_ref[...] = grad[:, :EMB]
    for t in range(TABLES):
        ahead, other = (t // 2 - yy) & 3, (t % 2) ^ half
        sent_ref[ahead, other, 0:BLOCK, :] = grad[:, (t + 1) * EMB:(t + 2) * EMB]
        sent_ref[ahead, other, BLOCK:BLOCK + META, :] = meta_ref[t]


def weight_kernel(pack_ref, cols_ref, other_ref, out_ref):
    yy = spot("y")
    for d in range(NY):
        to = (yy + d) & 3
        s = slice(d * 128, (d + 1) * 128)
        left = jnp.concatenate([cols_ref[:, s], other_ref[:, 2 * FEATURES + d * 128:2 * FEATURES + (d + 1) * 128]], axis=0)

        def put(first):
            right = jnp.concatenate([pack_ref[:, first:first + FEATURES], other_ref[:, first:first + FEATURES]], axis=0)
            out_ref[to] = dot(left, right, 0, 0).astype(BF16)

        pl.when(to < 2)(functools.partial(put, 0))
        pl.when(to >= 2)(functools.partial(put, FEATURES))


def add_kernel(in_ref, out_ref):
    total = in_ref[0].astype(F32)
    for i in range(1, in_ref.shape[0]):
        total = total + in_ref[i].astype(F32)
    if len(out_ref.shape) == 2:
        out_ref[...] = total.astype(out_ref.dtype)
    else:
        size = out_ref.shape[1]
        for i in range(out_ref.shape[0]):
            out_ref[i] = total[i * size:(i + 1) * size].astype(out_ref.dtype)


def expand(place, refs, look_ref, row_ref):
    lane_group = iota((8, 128), 1) // SLOTS
    sample_iota = iota((BLOCK, 128), 0)
    meta_row = iota((META, 128), 0)
    for j, ref in enumerate(refs):
        looks, rows = [], []
        for m in range(NY):
            b = m * (BLOCK + META)
            meta = ref[b + BLOCK:b + BLOCK + META, :].astype(F32)
            high = jnp.sum(jnp.where(meta_row == place * 2, meta, 0.0), axis=0, keepdims=True).astype(I32)
            low = jnp.sum(jnp.where(meta_row == place * 2 + 1, meta, 0.0), axis=0, keepdims=True).astype(I32) + 256
            pick = (sample_iota == (low & 127)).astype(F32).astype(BF16)
            looks.append(dot(pick, ref[b:b + BLOCK, :], 0, 0).astype(BF16))
            rows.append(jnp.broadcast_to((high * 4 + (low >> 7)).astype(F32), (8, 128)))
        for d in range(NX):
            row = rows[d]
            for g in range(NX):
                m = (d - g) % NX
                look_ref[d, j, g * SLOTS:(g + 1) * SLOTS, :] = looks[m][g * SLOTS:(g + 1) * SLOTS]
                if g:
                    row = jnp.where(lane_group == g, rows[m], row)
            row_ref[d, j] = row


def scatter(d, looks, rows, out_ref, first=None):
    base = iota((256, 128), 0).astype(F32)
    look = jnp.concatenate([ref[d].reshape(-1, EMB) for ref in looks], axis=0)
    for i in range(ROWS // 256):
        here = base + float(i * 256)
        s = slice(i * 256, (i + 1) * 256)
        hot = jnp.concatenate([(here == ref[d, j, 0:1, :]).astype(BF16) for ref in rows for j in range(ref.shape[1])], axis=1)
        total = dot(hot, look, 1, 0)
        if first is not None:
            total = total + first[s].astype(F32)
        out_ref[s] = total.astype(BF16)


def expand_kernel(count, *refs):
    place = spot("zl") * 2 + spot("c")
    look_own, row_own, look_other, row_other = refs[count:]
    expand(place ^ 1, refs[:count], look_other, row_other)
    expand(place, refs[:count], look_own, row_own)


def scatter_kernel(ds, parts, *refs):
    looks, rows, rest = refs[:parts], refs[parts:2 * parts], refs[2 * parts:]
    count = len(ds)
    firsts, outs = rest[:-count], rest[-count:]
    for i, d in enumerate(ds):
        scatter(d, looks, rows, outs[i], firsts[i] if firsts else None)


def update_kernel(a_ref, b_ref, c_ref, d_ref, table_ref, accum_ref, table_out, accum_out):
    eye = iota((128, 128), 0) == iota((128, 128), 1)
    for i in range(ROWS // 128):
        s = slice(i * 128, (i + 1) * 128)
        grad = a_ref[s].astype(F32) + b_ref[s].astype(F32)
        grad = grad + (c_ref[s].astype(F32) + d_ref[s].astype(F32))
        mean = jnp.sum(grad * grad, axis=1, keepdims=True) * (1.0 / EMB)
        old = jnp.sum(jnp.where(eye, accum_ref[i:i + 1, :], 0.0), axis=1, keepdims=True)
        new = old + mean
        table_out[s] = table_ref[s] - grad * (RATE / (jnp.sqrt(new) + EPSILON))
        accum_out[i:i + 1, :] = jnp.sum(jnp.where(eye, new, 0.0), axis=0, keepdims=True)


def ring(size, shift):
    return [(i, (i + shift) % size) for i in range(size)]


def shape(dims, kind):
    return jax.ShapeDtypeStruct(dims, kind)


def per_device(inputs, cotangent, cross_down, cross_up, cross_bias, indices, emb_table, row_accum):
    swap = ring(NC, 1)
    idx = jnp.transpose(indices, (1, 2, 0)).reshape(TABLES * HOT, BLOCK)

    def call(kernel, name, outs, operands, mib, work):
        return pl.pallas_call(
            kernel,
            out_shape=outs,
            in_specs=[VMEM] * len(operands),
            out_specs=(VMEM,) * len(outs) if isinstance(outs, tuple) else VMEM,
            compiler_params=params(mib),
            cost_estimate=work,
            name=name,
        )(*operands)

    meta = call(rank_kernel, "rank", shape((TABLES, META, 128), BF16), (idx,), 16, cost(2_000_000_000, 100_000))
    (inputs, cotangent, cross_down, cross_up), meta = lax.optimization_barrier(((inputs, cotangent, cross_down, cross_up), meta))
    pack, cols, both = call(
        hidden_kernel, "hidden",
        (shape((BLOCK, PACK), BF16), shape((BLOCK, RANK), BF16), shape((BLOCK, 2 * RANK), BF16)),
        (inputs, cotangent, cross_down, cross_up), 16, cost(500_000_000, 4_000_000),
    )
    dense_part, sent = call(
        pooled_kernel, "pooled",
        (shape((BLOCK, EMB), BF16), shape((NY, NZH, BLOCK + META, EMB), BF16)),
        (cotangent, both, cross_down, cross_up, cross_bias.reshape(FEATURES // 128, 128), meta),
        16, cost(300_000_000, 4_000_000),
    )

    other_pack = lax.ppermute(pack, "c", swap)
    along = [sent[0]] + [lax.ppermute(sent[d], "y", ring(NY, d)) for d in range(1, NY)]
    terms = call(
        weight_kernel, "weights", shape((NY, 128, FEATURES), BF16), (pack, cols, other_pack), 16, cost(300_000_000, 3_000_000)
    )
    along, _ = lax.optimization_barrier((along, terms))
    near = jnp.concatenate([v[0] for v in along], axis=0)
    far = jnp.concatenate([v[1] for v in along], axis=0)

    def cross(m):
        return lax.ppermute(far, ("zh", "zl"), [(i, (7 - i) ^ m) for i in range(8)])

    def line(m):
        return lax.ppermute(near, "zl", [(i, i ^ m) for i in range(NZL)])

    blocks = [near, cross(3), line(3), cross(2), line(2), cross(0), cross(1), line(1)]

    def exchanged(v, axes):
        return lax.all_to_all(v, axes, split_axis=0, concat_axis=0, tiled=True)

    def added(v, dims, kind):
        return call(add_kernel, "add", shape(dims, kind), (v,), 16, cost(1_000, 1_000))

    def expanded(blocks):
        look = shape((NX, len(blocks), 128, EMB), BF16)
        row = shape((NX, len(blocks), 8, 128), F32)
        return call(
            functools.partial(expand_kernel, len(blocks)), "expand", (look, row, look, row), tuple(blocks), 16, cost(1_000, 1_000)
        )

    lists = [expanded(blocks[:3])]
    lists[0], terms = lax.optimization_barrier((lists[0], exchanged(terms, "y")))
    terms = added(terms, (32, 4, FEATURES), BF16)
    late, _ = lax.optimization_barrier((blocks[3:6], terms))
    weight_total = added(exchanged(terms, ("zh", "zl", "x")), (4, FEATURES), F32)
    lists += [expanded(late), expanded(blocks[6:])]
    own, other = [[v[i] for v in lists] + [v[i + 1] for v in lists] for i in (0, 2)]

    def scattered(arrays, ds, firsts=()):
        return call(
            functools.partial(scatter_kernel, ds, len(lists)), "scatter",
            (shape((ROWS, EMB), BF16),) * len(ds), (*arrays, *firsts), 24, cost(1_000, 1_000),
        )

    def swapped(vs):
        return [lax.ppermute(v, "c", swap) for v in vs]

    first = scattered(other, (2,))
    other, first = lax.optimization_barrier((other, first))
    (first,) = swapped(first)
    second = scattered(other, (1, 3))
    other, second = lax.optimization_barrier((other, second))
    second = swapped(second)
    last = scattered(other, (0,))
    own, last = lax.optimization_barrier((own, last))
    (last,) = swapped(last)
    apart = scattered(own, (2,), (first,))
    own, apart = lax.optimization_barrier((own, apart))
    apart = lax.ppermute(apart[0], "x", ring(NX, 2))
    right, left = scattered(own, (1, 3), second)
    own, right, left = lax.optimization_barrier((own, right, left))
    right = lax.ppermute(right, "x", ring(NX, 1))
    left = lax.ppermute(left, "x", ring(NX, 3))
    (here,) = scattered(own, (0,), (last,))

    table_new, accum_new = call(
        update_kernel, "update", (shape((ROWS, EMB), F32), shape((8, 128), F32)),
        (here, right, left, apart, emb_table, row_accum.reshape(8, 128)), 16, cost(1_000, 1_000),
    )
    return (table_new, accum_new.reshape(ROWS), dense_part, weight_total)


def solution(mesh):
    fine = Mesh(mesh.devices.reshape(NY, NZH, NX, NC, NZL), AXES)
    in_specs = (
        P(AXES, None), P(AXES, None), P(), P(), P(), P(AXES, None, None), P(AXES, None), P(AXES),
    )
    out_specs = (P(AXES, None), P(AXES), P(AXES, None), P(AXES, None))
    return jax.shard_map(per_device, mesh=fine, in_specs=in_specs, out_specs=out_specs, check_vma=False)
```

```python
import functools

import jax
import jax.numpy as jnp
from jax import lax
from jax.experimental import pallas as pl
from jax.experimental.pallas import tpu as pltpu
from jax.sharding import Mesh, PartitionSpec as P

EMB = 128
TABLES = 8
HOT = 8
RANK = 512
FEATURES = 1152
RATE = 0.1
EPSILON = 1e-08
BLOCK = 128
ROWS = 1024
SLOTS = 32
META = 16
AXES = ("y", "zh", "x", "c", "zl")
NY, NZH, NX, NC, NZL = 4, 2, 4, 2, 4
PACK = 2 * FEATURES + RANK
VMEM = pl.BlockSpec(memory_space=pltpu.VMEM)
BF16, F32, I32 = jnp.bfloat16, jnp.float32, jnp.int32


def dot(a, b, left, right):
    return lax.dot_general(a, b, (((left,), (right,)), ((), ())), preferred_element_type=F32)


def iota(shape, dim):
    return lax.broadcasted_iota(I32, shape, dim)


def params(mib):
    return pltpu.CompilerParams(vmem_limit_bytes=mib * 1024 * 1024)


def cost(flops, bytes_accessed):
    return pl.CostEstimate(flops=flops, bytes_accessed=bytes_accessed, transcendentals=0)


def spot(axis):
    return lax.axis_index(axis)


def rank_kernel(idx_ref, meta_ref):
    yy, xx = spot("y"), spot("x")
    upper = (iota((128, 128), 0) < iota((128, 128), 1)).astype(BF16)
    ones = jnp.ones((128, 128), BF16)
    sub32 = iota((32, 128), 0)
    sub128 = iota((128, 128), 0)
    pair = iota((META, 128), 0) // 2
    second = iota((META, 128), 0) % 2 == 1
    for t in range(TABLES):
        ahead = (t // 2 - yy) & 3
        idx = idx_ref[t * HOT:(t + 1) * HOT, :]
        owner = idx >> 10
        place = (owner & 3) * 2 + ((owner >> 2) & 1)
        group = ((owner >> 3) - xx - ahead) & 3
        full = place * 4 + group
        high = ((idx >> 2) & 255).astype(F32)
        low = ((idx & 3) * 128 + iota((HOT, 128), 1) - 256).astype(F32)
        hot = jnp.concatenate([(sub32 == full[k:k + 1]).astype(F32) for k in range(HOT)], axis=0)
        hot16 = hot.astype(BF16)
        before = dot(hot16, upper, 1, 0)
        total = dot(hot16, ones, 1, 0)
        base = jnp.zeros((32, 128), F32)
        slots, values = [], []
        for k in range(HOT):
            s = slice(k * 32, (k + 1) * 32)
            rank = jnp.sum(hot[s] * (before[s] + base), axis=0, keepdims=True).astype(I32)
            base = base + total[s]
            slots.append((sub128 == group[k:k + 1] * SLOTS + rank).astype(F32).astype(BF16))
            value = jnp.where(second, low[k:k + 1], high[k:k + 1])
            values.append(jnp.where(pair == place[k:k + 1], value, 0.0).astype(BF16))
        meta = dot(jnp.concatenate(values, axis=1), jnp.concatenate(slots, axis=1), 1, 1)
        meta_ref[t] = meta.astype(BF16)


def hidden_kernel(in_ref, cot_ref, down_ref, up_ref, pack_ref, cols_ref, both_ref):
    yy, core = spot("y"), spot("c")
    inputs = in_ref[...]
    grad_scale = (cot_ref[...].astype(F32) * inputs.astype(F32)).astype(BF16)
    pack_ref[:, :FEATURES] = inputs
    pack_ref[:, FEATURES:2 * FEATURES] = grad_scale
    hidden = dot(inputs, down_ref[...], 1, 0).astype(BF16)
    grad_hidden = dot(grad_scale, up_ref[...], 1, 1).astype(BF16)
    both_ref[:, :RANK] = grad_hidden
    both_ref[:, RANK:] = hidden

    both = jnp.concatenate([grad_hidden, hidden], axis=1)
    src = iota((2 * RANK, RANK), 0)
    dst = iota((2 * RANK, RANK), 1)
    from_y = ((dst >> 7) + yy) & 3
    want = from_y * 256 + ((dst >> 6) & 1) * 128 + ((dst >> 2) & 3) * 32 + ((dst >> 4) & 3) * 4 + (dst & 3)
    pack_ref[:, 2 * FEATURES:] = dot(both, (src == want + (1 - core) * 16).astype(F32).astype(BF16), 1, 0).astype(BF16)
    cols_ref[...] = dot(both, (src == want + core * 16).astype(F32).astype(BF16), 1, 0).astype(BF16)


def pooled_kernel(cot_ref, both_ref, down_ref, up_ref, bias_ref, meta_ref, dense_ref, sent_ref):
    yy, half = spot("y"), spot("zh")
    bias = jnp.concatenate([bias_ref[i:i + 1, :] for i in range(FEATURES // 128)], axis=1)
    scale = dot(both_ref[:, RANK:], up_ref[...], 1, 0) + bias
    back = dot(both_ref[:, :RANK], down_ref[...], 1, 1)
    grad = (cot_ref[...].astype(F32) * (scale + 1.0) + back).astype(BF16)
    dense_ref[...] = grad[:, :EMB]
    for t in range(TABLES):
        ahead, other = (t // 2 - yy) & 3, (t % 2) ^ half
        sent_ref[ahead, other, 0:BLOCK, :] = grad[:, (t + 1) * EMB:(t + 2) * EMB]
        sent_ref[ahead, other, BLOCK:BLOCK + META, :] = meta_ref[t]


def weight_kernel(pack_ref, cols_ref, other_ref, out_ref):
    yy = spot("y")
    for d in range(NY):
        to = (yy + d) & 3
        s = slice(d * 128, (d + 1) * 128)
        left = jnp.concatenate([cols_ref[:, s], other_ref[:, 2 * FEATURES + d * 128:2 * FEATURES + (d + 1) * 128]], axis=0)

        def put(first):
            right = jnp.concatenate([pack_ref[:, first:first + FEATURES], other_ref[:, first:first + FEATURES]], axis=0)
            out_ref[to] = dot(left, right, 0, 0).astype(BF16)

        pl.when(to < 2)(functools.partial(put, 0))
        pl.when(to >= 2)(functools.partial(put, FEATURES))


def add_kernel(in_ref, out_ref):
    total = in_ref[0].astype(F32)
    for i in range(1, in_ref.shape[0]):
        total = total + in_ref[i].astype(F32)
    if len(out_ref.shape) == 2:
        out_ref[...] = total.astype(out_ref.dtype)
    else:
        size = out_ref.shape[1]
        for i in range(out_ref.shape[0]):
            out_ref[i] = total[i * size:(i + 1) * size].astype(out_ref.dtype)


def expand(place, refs, look_ref, row_ref):
    lane_group = iota((8, 128), 1) // SLOTS
    sample_iota = iota((BLOCK, 128), 0)
    meta_row = iota((META, 128), 0)
    for j, ref in enumerate(refs):
        looks, rows = [], []
        for m in range(NY):
            b = m * (BLOCK + META)
            meta = ref[b + BLOCK:b + BLOCK + META, :].astype(F32)
            high = jnp.sum(jnp.where(meta_row == place * 2, meta, 0.0), axis=0, keepdims=True).astype(I32)
            low = jnp.sum(jnp.where(meta_row == place * 2 + 1, meta, 0.0), axis=0, keepdims=True).astype(I32) + 256
            pick = (sample_iota == (low & 127)).astype(F32).astype(BF16)
            looks.append(dot(pick, ref[b:b + BLOCK, :], 0, 0).astype(BF16))
            rows.append(jnp.broadcast_to((high * 4 + (low >> 7)).astype(F32), (8, 128)))
        for d in range(NX):
            row = rows[d]
            for g in range(NX):
                m = (d - g) % NX
                look_ref[d, j, g * SLOTS:(g + 1) * SLOTS, :] = looks[m][g * SLOTS:(g + 1) * SLOTS]
                if g:
                    row = jnp.where(lane_group == g, rows[m], row)
            row_ref[d, j] = row


def scatter(d, looks, rows, out_ref, firsts=()):
    base = iota((256, 128), 0).astype(F32)
    look = jnp.concatenate([ref[d].reshape(-1, EMB) for ref in looks], axis=0)
    for i in range(ROWS // 256):
        here = base + float(i * 256)
        s = slice(i * 256, (i + 1) * 256)
        hot = jnp.concatenate([(here == ref[d, j, 0:1, :]).astype(BF16) for ref in rows for j in range(ref.shape[1])], axis=1)
        total = dot(hot, look, 1, 0)
        for first in firsts:
            total = total + first[s].astype(F32)
        out_ref[s] = total.astype(out_ref.dtype)


def expand_kernel(count, *refs):
    place = spot("zl") * 2 + spot("c")
    look_own, row_own, look_other, row_other = refs[count:]
    expand(place ^ 1, refs[:count], look_other, row_other)
    expand(place, refs[:count], look_own, row_own)


def scatter_kernel(ds, *refs):
    look, row, rest = refs[0], refs[1], refs[2:]
    count = len(ds)
    firsts, outs = rest[:-count], rest[-count:]
    for i, d in enumerate(ds):
        scatter(d, (look,), (row,), outs[i], firsts[i::count])


def update_kernel(a_ref, b_ref, c_ref, d_ref, table_ref, accum_ref, table_out, accum_out):
    eye = iota((128, 128), 0) == iota((128, 128), 1)
    for i in range(ROWS // 128):
        s = slice(i * 128, (i + 1) * 128)
        grad = a_ref[s].astype(F32) + b_ref[s].astype(F32)
        grad = grad + (c_ref[s].astype(F32) + d_ref[s].astype(F32))
        mean = jnp.sum(grad * grad, axis=1, keepdims=True) * (1.0 / EMB)
        old = jnp.sum(jnp.where(eye, accum_ref[i:i + 1, :], 0.0), axis=1, keepdims=True)
        new = old + mean
        table_out[s] = table_ref[s] - grad * (RATE / (jnp.sqrt(new) + EPSILON))
        accum_out[i:i + 1, :] = jnp.sum(jnp.where(eye, new, 0.0), axis=0, keepdims=True)


def ring(size, shift):
    return [(i, (i + shift) % size) for i in range(size)]


def shape(dims, kind):
    return jax.ShapeDtypeStruct(dims, kind)


def per_device(inputs, cotangent, cross_down, cross_up, cross_bias, indices, emb_table, row_accum):
    swap = ring(NC, 1)
    idx = jnp.transpose(indices, (1, 2, 0)).reshape(TABLES * HOT, BLOCK)

    def call(kernel, name, outs, operands, mib, work):
        return pl.pallas_call(
            kernel,
            out_shape=outs,
            in_specs=[VMEM] * len(operands),
            out_specs=(VMEM,) * len(outs) if isinstance(outs, tuple) else VMEM,
            compiler_params=params(mib),
            cost_estimate=work,
            name=name,
        )(*operands)

    meta = call(rank_kernel, "rank", shape((TABLES, META, 128), BF16), (idx,), 16, cost(2_000_000_000, 100_000))
    (inputs, cotangent, cross_down, cross_up), meta = lax.optimization_barrier(((inputs, cotangent, cross_down, cross_up), meta))
    pack, cols, both = call(
        hidden_kernel, "hidden",
        (shape((BLOCK, PACK), BF16), shape((BLOCK, RANK), BF16), shape((BLOCK, 2 * RANK), BF16)),
        (inputs, cotangent, cross_down, cross_up), 16, cost(500_000_000, 4_000_000),
    )
    dense_part, sent = call(
        pooled_kernel, "pooled",
        (shape((BLOCK, EMB), BF16), shape((NY, NZH, BLOCK + META, EMB), BF16)),
        (cotangent, both, cross_down, cross_up, cross_bias.reshape(FEATURES // 128, 128), meta),
        16, cost(300_000_000, 4_000_000),
    )

    other_pack = lax.ppermute(pack, "c", swap)
    along = [sent[0]] + [lax.ppermute(sent[d], "y", ring(NY, d)) for d in range(1, NY)]
    terms = call(
        weight_kernel, "weights", shape((NY, 128, FEATURES), BF16), (pack, cols, other_pack), 16, cost(300_000_000, 3_000_000)
    )
    along, _ = lax.optimization_barrier((along, terms))
    near = jnp.concatenate([v[0] for v in along], axis=0)
    far = jnp.concatenate([v[1] for v in along], axis=0)

    def cross(m):
        return lax.ppermute(far, ("zh", "zl"), [(i, (7 - i) ^ m) for i in range(8)])

    def line(m):
        return lax.ppermute(near, "zl", [(i, i ^ m) for i in range(NZL)])

    def pass_on(v):
        return lax.ppermute(v, "zl", [(i, i ^ 1) for i in range(NZL)])

    sent_on = [cross(2), cross(0), line(2)]
    blocks = [near] + sent_on + [line(1)]
    passed = [pass_on(v) for v in sent_on]

    def exchanged(v, axes):
        return lax.all_to_all(v, axes, split_axis=0, concat_axis=0, tiled=True)

    def added(v, dims, kind):
        return call(add_kernel, "add", shape(dims, kind), (v,), 16, cost(1_000, 1_000))

    def expanded(blocks):
        look = shape((NX, len(blocks), 128, EMB), BF16)
        row = shape((NX, len(blocks), 8, 128), F32)
        return call(
            functools.partial(expand_kernel, len(blocks)), "expand", (look, row, look, row), tuple(blocks), 16, cost(1_000, 1_000)
        )

    def scattered(arrays, ds, firsts=(), kind=BF16):
        return call(
            functools.partial(scatter_kernel, ds), "scatter",
            (shape((ROWS, EMB), kind),) * len(ds), (*arrays, *firsts), 24, cost(1_000, 1_000),
        )

    def swapped(vs):
        return [lax.ppermute(v, "c", swap) for v in vs]

    early = expanded(blocks)
    early, terms = lax.optimization_barrier((early, exchanged(terms, "y")))
    terms = added(terms, (32, 4, FEATURES), BF16)
    weight_total = added(exchanged(terms, ("zh", "zl", "x")), (4, FEATURES), F32)
    order = (2, 1, 3, 0)
    base_own = scattered(early[:2], order, kind=F32)
    base_other = scattered(early[2:], order, kind=F32)
    late, base_own, base_other, _ = lax.optimization_barrier((passed, base_own, base_other, terms))
    late = expanded(late)
    own, other = late[:2], late[2:]

    first = scattered(other, (2,), base_other[:1])
    other, first = lax.optimization_barrier((other, first))
    (first,) = swapped(first)
    rest = scattered(other, (1, 3, 0), base_other[1:])
    own, rest = lax.optimization_barrier((own, rest))
    rest = swapped(rest)
    apart = scattered(own, (2,), (base_own[0], first))
    own, apart = lax.optimization_barrier((own, apart))
    apart = lax.ppermute(apart[0], "x", ring(NX, 2))
    right, left = scattered(own, (1, 3), (*base_own[1:3], *rest[:2]))
    own, right, left = lax.optimization_barrier((own, right, left))
    right = lax.ppermute(right, "x", ring(NX, 1))
    left = lax.ppermute(left, "x", ring(NX, 3))
    (here,) = scattered(own, (0,), (base_own[3], rest[2]))

    table_new, accum_new = call(
        update_kernel, "update", (shape((ROWS, EMB), F32), shape((8, 128), F32)),
        (here, right, left, apart, emb_table, row_accum.reshape(8, 128)), 16, cost(1_000, 1_000),
    )
    return (table_new, accum_new.reshape(ROWS), dense_part, weight_total)


def solution(mesh):
    fine = Mesh(mesh.devices.reshape(NY, NZH, NX, NC, NZL), AXES)
    in_specs = (
        P(AXES, None), P(AXES, None), P(), P(), P(), P(AXES, None, None), P(AXES, None), P(AXES),
    )
    out_specs = (P(AXES, None), P(AXES), P(AXES, None), P(AXES, None))
    return jax.shard_map(per_device, mesh=fine, in_specs=in_specs, out_specs=out_specs, check_vma=False)
```

```python
import functools

import jax
import jax.numpy as jnp
from jax import lax
from jax.experimental import pallas as pl
from jax.experimental.pallas import tpu as pltpu
from jax.sharding import Mesh, PartitionSpec as P

EMB = 128
TABLES = 8
HOT = 8
RANK = 512
FEATURES = 1152
RATE = 0.1
EPSILON = 1e-08
BLOCK = 128
ROWS = 1024
SLOTS = 32
META = 16
AXES = ("y", "zh", "x", "c", "zl")
NY, NZH, NX, NC, NZL = 4, 2, 4, 2, 4
PACK = 2 * FEATURES + RANK
VMEM = pl.BlockSpec(memory_space=pltpu.VMEM)
BF16, F32, I32 = jnp.bfloat16, jnp.float32, jnp.int32


def dot(a, b, left, right):
    return lax.dot_general(a, b, (((left,), (right,)), ((), ())), preferred_element_type=F32)


def iota(shape, dim):
    return lax.broadcasted_iota(I32, shape, dim)


def params(mib):
    return pltpu.CompilerParams(vmem_limit_bytes=mib * 1024 * 1024)


def cost(flops, bytes_accessed):
    return pl.CostEstimate(flops=flops, bytes_accessed=bytes_accessed, transcendentals=0)


def spot(axis):
    return lax.axis_index(axis)


def rank_kernel(idx_ref, meta_ref):
    yy, xx = spot("y"), spot("x")
    upper = (iota((128, 128), 0) < iota((128, 128), 1)).astype(BF16)
    ones = jnp.ones((128, 128), BF16)
    sub32 = iota((32, 128), 0)
    sub128 = iota((128, 128), 0)
    pair = iota((META, 128), 0) // 2
    second = iota((META, 128), 0) % 2 == 1
    for t in range(TABLES):
        ahead = (t // 2 - yy) & 3
        idx = idx_ref[t * HOT:(t + 1) * HOT, :]
        owner = idx >> 10
        place = (owner & 3) * 2 + ((owner >> 2) & 1)
        group = ((owner >> 3) - xx - ahead) & 3
        full = place * 4 + group
        high = ((idx >> 2) & 255).astype(F32)
        low = ((idx & 3) * 128 + iota((HOT, 128), 1) - 256).astype(F32)
        hot = jnp.concatenate([(sub32 == full[k:k + 1]).astype(F32) for k in range(HOT)], axis=0)
        hot16 = hot.astype(BF16)
        before = dot(hot16, upper, 1, 0)
        total = dot(hot16, ones, 1, 0)
        base = jnp.zeros((32, 128), F32)
        slots, values = [], []
        for k in range(HOT):
            s = slice(k * 32, (k + 1) * 32)
            rank = jnp.sum(hot[s] * (before[s] + base), axis=0, keepdims=True).astype(I32)
            base = base + total[s]
            slots.append((sub128 == group[k:k + 1] * SLOTS + rank).astype(F32).astype(BF16))
            value = jnp.where(second, low[k:k + 1], high[k:k + 1])
            values.append(jnp.where(pair == place[k:k + 1], value, 0.0).astype(BF16))
        meta = dot(jnp.concatenate(values, axis=1), jnp.concatenate(slots, axis=1), 1, 1)
        meta_ref[t] = meta.astype(BF16)


def hidden_kernel(in_ref, cot_ref, down_ref, up_ref, pack_ref, cols_ref, both_ref):
    core = spot("c")
    inputs = in_ref[...]
    grad_scale = (cot_ref[...].astype(F32) * inputs.astype(F32)).astype(BF16)
    pack_ref[:, :FEATURES] = inputs
    pack_ref[:, FEATURES:2 * FEATURES] = grad_scale
    hidden = dot(inputs, down_ref[...], 1, 0).astype(BF16)
    grad_hidden = dot(grad_scale, up_ref[...], 1, 1).astype(BF16)
    both_ref[:, :RANK] = grad_hidden
    both_ref[:, RANK:] = hidden

    both = jnp.concatenate([grad_hidden, hidden], axis=1)
    src = iota((2 * RANK, RANK), 0)
    dst = iota((2 * RANK, RANK), 1)
    want = (dst >> 7) * 256 + ((dst >> 6) & 1) * 128 + ((dst >> 2) & 3) * 32 + ((dst >> 4) & 3) * 4 + (dst & 3)
    pack_ref[:, 2 * FEATURES:] = dot(both, (src == want + (1 - core) * 16).astype(F32).astype(BF16), 1, 0).astype(BF16)
    cols_ref[...] = dot(both, (src == want + core * 16).astype(F32).astype(BF16), 1, 0).astype(BF16)


def pooled_kernel(cot_ref, both_ref, down_ref, up_ref, bias_ref, meta_ref, dense_ref, sent_ref):
    yy, half = spot("y"), spot("zh")
    bias = jnp.concatenate([bias_ref[i:i + 1, :] for i in range(FEATURES // 128)], axis=1)
    scale = dot(both_ref[:, RANK:], up_ref[...], 1, 0) + bias
    back = dot(both_ref[:, :RANK], down_ref[...], 1, 1)
    grad = (cot_ref[...].astype(F32) * (scale + 1.0) + back).astype(BF16)
    dense_ref[...] = grad[:, :EMB]
    for t in range(TABLES):
        ahead, other = (t // 2 - yy) & 3, (t % 2) ^ half
        sent_ref[ahead, other, 0:BLOCK, :] = grad[:, (t + 1) * EMB:(t + 2) * EMB]
        sent_ref[ahead, other, BLOCK:BLOCK + META, :] = meta_ref[t]


def weight_kernel(pack_ref, cols_ref, other_ref, out_ref):
    for half in range(2):
        s = slice(half * 256, (half + 1) * 256)
        t = slice(half * FEATURES, (half + 1) * FEATURES)
        theirs = other_ref[:, 2 * FEATURES + half * 256:2 * FEATURES + (half + 1) * 256]
        left = jnp.concatenate([cols_ref[:, s], theirs], axis=0)
        right = jnp.concatenate([pack_ref[:, t], other_ref[:, t]], axis=0)
        out_ref[half * 2:half * 2 + 2] = dot(left, right, 0, 0).astype(BF16).reshape(2, 128, FEATURES)


def add_kernel(in_ref, out_ref):
    total = in_ref[0].astype(F32)
    for i in range(1, in_ref.shape[0]):
        total = total + in_ref[i].astype(F32)
    if len(out_ref.shape) == 2:
        out_ref[...] = total.astype(out_ref.dtype)
    else:
        size = out_ref.shape[1]
        for i in range(out_ref.shape[0]):
            out_ref[i] = total[i * size:(i + 1) * size].astype(out_ref.dtype)


def expand(place, refs, look_ref, row_ref):
    lane_group = iota((8, 128), 1) // SLOTS
    sample_iota = iota((BLOCK, 128), 0)
    meta_row = iota((META, 128), 0)
    for j, ref in enumerate(refs):
        looks, rows = [], []
        for m in range(NY):
            b = m * (BLOCK + META)
            meta = ref[b + BLOCK:b + BLOCK + META, :].astype(F32)
            high = jnp.sum(jnp.where(meta_row == place * 2, meta, 0.0), axis=0, keepdims=True).astype(I32)
            low = jnp.sum(jnp.where(meta_row == place * 2 + 1, meta, 0.0), axis=0, keepdims=True).astype(I32) + 256
            pick = (sample_iota == (low & 127)).astype(F32).astype(BF16)
            looks.append(dot(pick, ref[b:b + BLOCK, :], 0, 0).astype(BF16))
            rows.append(jnp.broadcast_to((high * 4 + (low >> 7)).astype(F32), (8, 128)))
        for d in range(NX):
            row = rows[d]
            for g in range(NX):
                m = (d - g) % NX
                look_ref[d, j, g * SLOTS:(g + 1) * SLOTS, :] = looks[m][g * SLOTS:(g + 1) * SLOTS]
                if g:
                    row = jnp.where(lane_group == g, rows[m], row)
            row_ref[d, j] = row


def scatter(d, looks, rows, out_ref, firsts=()):
    base = iota((256, 128), 0).astype(F32)
    look = jnp.concatenate([ref[d].reshape(-1, EMB) for ref in looks], axis=0)
    for i in range(ROWS // 256):
        here = base + float(i * 256)
        s = slice(i * 256, (i + 1) * 256)
        hot = jnp.concatenate([(here == ref[d, j, 0:1, :]).astype(BF16) for ref in rows for j in range(ref.shape[1])], axis=1)
        total = dot(hot, look, 1, 0)
        for first in firsts:
            total = total + first[s].astype(F32)
        out_ref[s] = total.astype(out_ref.dtype)


def expand_kernel(count, *refs):
    place = spot("zl") * 2 + spot("c")
    look_own, row_own, look_other, row_other = refs[count:]
    expand(place ^ 1, refs[:count], look_other, row_other)
    expand(place, refs[:count], look_own, row_own)


def scatter_kernel(ds, *refs):
    looks, rows, rest = refs[0:4:2], refs[1:4:2], refs[4:]
    count = len(ds)
    firsts, outs = rest[:-count], rest[-count:]
    for i, d in enumerate(ds):
        scatter(d, looks, rows, outs[i], firsts[i::count])


def update_kernel(a_ref, b_ref, c_ref, d_ref, table_ref, accum_ref, table_out, accum_out):
    eye = iota((128, 128), 0) == iota((128, 128), 1)
    for i in range(ROWS // 128):
        s = slice(i * 128, (i + 1) * 128)
        grad = a_ref[s].astype(F32) + b_ref[s].astype(F32)
        grad = grad + (c_ref[s].astype(F32) + d_ref[s].astype(F32))
        mean = jnp.sum(grad * grad, axis=1, keepdims=True) * (1.0 / EMB)
        old = jnp.sum(jnp.where(eye, accum_ref[i:i + 1, :], 0.0), axis=1, keepdims=True)
        new = old + mean
        table_out[s] = table_ref[s] - grad * (RATE / (jnp.sqrt(new) + EPSILON))
        accum_out[i:i + 1, :] = jnp.sum(jnp.where(eye, new, 0.0), axis=0, keepdims=True)


def ring(size, shift):
    return [(i, (i + shift) % size) for i in range(size)]


def shape(dims, kind):
    return jax.ShapeDtypeStruct(dims, kind)


def per_device(inputs, cotangent, cross_down, cross_up, cross_bias, indices, emb_table, row_accum):
    swap = ring(NC, 1)
    idx = jnp.transpose(indices, (1, 2, 0)).reshape(TABLES * HOT, BLOCK)

    def call(kernel, name, outs, operands, mib, work):
        return pl.pallas_call(
            kernel,
            out_shape=outs,
            in_specs=[VMEM] * len(operands),
            out_specs=(VMEM,) * len(outs) if isinstance(outs, tuple) else VMEM,
            compiler_params=params(mib),
            cost_estimate=work,
            name=name,
        )(*operands)

    meta = call(rank_kernel, "rank", shape((TABLES, META, 128), BF16), (idx,), 16, cost(2_000_000_000, 100_000))
    (inputs, cotangent, cross_down, cross_up), meta = lax.optimization_barrier(((inputs, cotangent, cross_down, cross_up), meta))
    pack, cols, both = call(
        hidden_kernel, "hidden",
        (shape((BLOCK, PACK), BF16), shape((BLOCK, RANK), BF16), shape((BLOCK, 2 * RANK), BF16)),
        (inputs, cotangent, cross_down, cross_up), 16, cost(500_000_000, 4_000_000),
    )
    dense_part, sent = call(
        pooled_kernel, "pooled",
        (shape((BLOCK, EMB), BF16), shape((NY, NZH, BLOCK + META, EMB), BF16)),
        (cotangent, both, cross_down, cross_up, cross_bias.reshape(FEATURES // 128, 128), meta),
        16, cost(300_000_000, 4_000_000),
    )

    other_pack = lax.ppermute(pack, "c", swap)
    along = [sent[0]] + [lax.ppermute(sent[d], "y", ring(NY, d)) for d in range(1, NY)]
    terms = call(
        weight_kernel, "weights", shape((NY, 128, FEATURES), BF16), (pack, cols, other_pack), 16, cost(300_000_000, 3_000_000)
    )
    along, _ = lax.optimization_barrier((along, terms))
    near = jnp.concatenate([v[0] for v in along], axis=0)
    far = jnp.concatenate([v[1] for v in along], axis=0)

    def cross(m):
        return lax.ppermute(far, ("zh", "zl"), [(i, (7 - i) ^ m) for i in range(8)])

    def line(m):
        return lax.ppermute(near, "zl", [(i, i ^ m) for i in range(NZL)])

    def pass_on(v):
        return lax.ppermute(v, "zl", [(i, i ^ 1) for i in range(NZL)])

    sent_on = [cross(2), cross(0), line(2)]
    blocks = [near] + sent_on + [line(1)]
    passed = [pass_on(v) for v in sent_on]

    def exchanged(v, axes):
        return lax.all_to_all(v, axes, split_axis=0, concat_axis=0, tiled=True)

    def added(v, dims, kind):
        return call(add_kernel, "add", shape(dims, kind), (v,), 16, cost(1_000, 1_000))

    def expanded(blocks):
        look = shape((NX, len(blocks), 128, EMB), BF16)
        row = shape((NX, len(blocks), 8, 128), F32)
        return call(
            functools.partial(expand_kernel, len(blocks)), "expand", (look, row, look, row), tuple(blocks), 16, cost(1_000, 1_000)
        )

    def scattered(arrays, ds, firsts=()):
        return call(
            functools.partial(scatter_kernel, ds), "scatter",
            (shape((ROWS, EMB), BF16),) * len(ds), (*arrays, *firsts), 24, cost(1_000, 1_000),
        )

    def swapped(vs):
        return [lax.ppermute(v, "c", swap) for v in vs]

    early = expanded(blocks)
    early, terms = lax.optimization_barrier((early, exchanged(terms, "y")))
    terms = added(terms, (32, 4, FEATURES), BF16)
    weight_total = added(exchanged(terms, ("zh", "zl", "x")), (4, FEATURES), F32)
    late, _ = lax.optimization_barrier((passed, terms))
    late = expanded(late)
    own, other = [*early[:2], *late[:2]], [*early[2:], *late[2:]]

    first = scattered(other, (2,))
    other, first = lax.optimization_barrier((other, first))
    (first,) = swapped(first)
    rest = scattered(other, (1, 3))
    own, rest = lax.optimization_barrier((own, rest))
    rest = swapped(rest)
    apart = scattered(own, (2,), (first,))
    own, apart = lax.optimization_barrier((own, apart))
    apart = lax.ppermute(apart[0], "x", ring(NX, 2))
    right, left = scattered(own, (1, 3), rest)
    other, right, left = lax.optimization_barrier((other, right, left))
    right = lax.ppermute(right, "x", ring(NX, 1))
    left = lax.ppermute(left, "x", ring(NX, 3))
    (here,) = scattered(own, (0,), swapped(scattered(other, (0,))))

    here, weight_total = lax.optimization_barrier((here, weight_total))

    table_new, accum_new = call(
        update_kernel, "update", (shape((ROWS, EMB), F32), shape((8, 128), F32)),
        (here, right, left, apart, emb_table, row_accum.reshape(8, 128)), 16, cost(1_000, 1_000),
    )
    return (table_new, accum_new.reshape(ROWS), dense_part, weight_total)


def solution(mesh):
    fine = Mesh(mesh.devices.reshape(NY, NZH, NX, NC, NZL), AXES)
    in_specs = (
        P(AXES, None), P(AXES, None), P(), P(), P(), P(AXES, None, None), P(AXES, None), P(AXES),
    )
    out_specs = (P(AXES, None), P(AXES), P(AXES, None), P(AXES, None))
    return jax.shard_map(per_device, mesh=fine, in_specs=in_specs, out_specs=out_specs, check_vma=False)
```

```python
import functools

import jax
import jax.numpy as jnp
from jax import lax
from jax.experimental import pallas as pl
from jax.experimental.pallas import tpu as pltpu
from jax.sharding import Mesh, PartitionSpec as P

EMB = 128
TABLES = 8
HOT = 8
RANK = 512
FEATURES = 1152
RATE = 0.1
EPSILON = 1e-08
BLOCK = 128
ROWS = 1024
SLOTS = 32
META = 16
AXES = ("y", "zh", "x", "c", "zl")
NY, NZH, NX, NC, NZL = 4, 2, 4, 2, 4
PACK = 2 * FEATURES + RANK
VMEM = pl.BlockSpec(memory_space=pltpu.VMEM)
BF16, F32, I32 = jnp.bfloat16, jnp.float32, jnp.int32


def dot(a, b, left, right):
    return lax.dot_general(a, b, (((left,), (right,)), ((), ())), preferred_element_type=F32)


def iota(shape, dim):
    return lax.broadcasted_iota(I32, shape, dim)


def params(mib):
    return pltpu.CompilerParams(vmem_limit_bytes=mib * 1024 * 1024)


def cost(flops, bytes_accessed):
    return pl.CostEstimate(flops=flops, bytes_accessed=bytes_accessed, transcendentals=0)


def spot(axis):
    return lax.axis_index(axis)


def rank_kernel(idx_ref, meta_ref):
    yy, xx = spot("y"), spot("x")
    upper = (iota((128, 128), 0) < iota((128, 128), 1)).astype(BF16)
    ones = jnp.ones((128, 128), BF16)
    sub32 = iota((32, 128), 0)
    sub128 = iota((128, 128), 0)
    pair = iota((META, 128), 0) // 2
    second = iota((META, 128), 0) % 2 == 1
    for t in range(TABLES):
        ahead = (t // 2 - yy) & 3
        idx = idx_ref[t * HOT:(t + 1) * HOT, :]
        owner = idx >> 10
        place = (owner & 3) * 2 + ((owner >> 2) & 1)
        group = ((owner >> 3) - xx - ahead) & 3
        full = place * 4 + group
        high = ((idx >> 2) & 255).astype(F32)
        low = ((idx & 3) * 128 + iota((HOT, 128), 1) - 256).astype(F32)
        hot = jnp.concatenate([(sub32 == full[k:k + 1]).astype(F32) for k in range(HOT)], axis=0)
        hot16 = hot.astype(BF16)
        before = dot(hot16, upper, 1, 0)
        total = dot(hot16, ones, 1, 0)
        base = jnp.zeros((32, 128), F32)
        slots, values = [], []
        for k in range(HOT):
            s = slice(k * 32, (k + 1) * 32)
            rank = jnp.sum(hot[s] * (before[s] + base), axis=0, keepdims=True).astype(I32)
            base = base + total[s]
            slots.append((sub128 == group[k:k + 1] * SLOTS + rank).astype(F32).astype(BF16))
            value = jnp.where(second, low[k:k + 1], high[k:k + 1])
            values.append(jnp.where(pair == place[k:k + 1], value, 0.0).astype(BF16))
        meta = dot(jnp.concatenate(values, axis=1), jnp.concatenate(slots, axis=1), 1, 1)
        meta_ref[t] = meta.astype(BF16)


def hidden_kernel(in_ref, cot_ref, down_ref, up_ref, pack_ref, cols_ref, both_ref):
    core = spot("c")
    inputs = in_ref[...]
    grad_scale = (cot_ref[...].astype(F32) * inputs.astype(F32)).astype(BF16)
    pack_ref[:, :FEATURES] = inputs
    pack_ref[:, FEATURES:2 * FEATURES] = grad_scale
    hidden = dot(inputs, down_ref[...], 1, 0).astype(BF16)
    grad_hidden = dot(grad_scale, up_ref[...], 1, 1).astype(BF16)
    both_ref[:, :RANK] = grad_hidden
    both_ref[:, RANK:] = hidden

    both = jnp.concatenate([grad_hidden, hidden], axis=1)
    src = iota((2 * RANK, RANK), 0)
    dst = iota((2 * RANK, RANK), 1)
    want = (dst >> 7) * 256 + ((dst >> 6) & 1) * 128 + ((dst >> 2) & 3) * 32 + ((dst >> 4) & 3) * 4 + (dst & 3)
    pack_ref[:, 2 * FEATURES:] = dot(both, (src == want + (1 - core) * 16).astype(F32).astype(BF16), 1, 0).astype(BF16)
    cols_ref[...] = dot(both, (src == want + core * 16).astype(F32).astype(BF16), 1, 0).astype(BF16)


def pooled_kernel(cot_ref, both_ref, down_ref, up_ref, bias_ref, meta_ref, dense_ref, sent_ref):
    yy, half = spot("y"), spot("zh")
    bias = jnp.concatenate([bias_ref[i:i + 1, :] for i in range(FEATURES // 128)], axis=1)
    scale = dot(both_ref[:, RANK:], up_ref[...], 1, 0) + bias
    back = dot(both_ref[:, :RANK], down_ref[...], 1, 1)
    grad = (cot_ref[...].astype(F32) * (scale + 1.0) + back).astype(BF16)
    dense_ref[...] = grad[:, :EMB]
    for t in range(TABLES):
        ahead, other = (t // 2 - yy) & 3, (t % 2) ^ half
        sent_ref[ahead, other, 0:BLOCK, :] = grad[:, (t + 1) * EMB:(t + 2) * EMB]
        sent_ref[ahead, other, BLOCK:BLOCK + META, :] = meta_ref[t]


def weight_kernel(pack_ref, cols_ref, other_ref, out_ref):
    for half in range(2):
        s = slice(half * 256, (half + 1) * 256)
        t = slice(half * FEATURES, (half + 1) * FEATURES)
        theirs = other_ref[:, 2 * FEATURES + half * 256:2 * FEATURES + (half + 1) * 256]
        left = jnp.concatenate([cols_ref[:, s], theirs], axis=0)
        right = jnp.concatenate([pack_ref[:, t], other_ref[:, t]], axis=0)
        out_ref[half * 2:half * 2 + 2] = dot(left, right, 0, 0).astype(BF16).reshape(2, 128, FEATURES)


def add_kernel(in_ref, out_ref):
    total = in_ref[0].astype(F32)
    for i in range(1, in_ref.shape[0]):
        total = total + in_ref[i].astype(F32)
    if len(out_ref.shape) == 2:
        out_ref[...] = total.astype(out_ref.dtype)
    else:
        size = out_ref.shape[1]
        for i in range(out_ref.shape[0]):
            out_ref[i] = total[i * size:(i + 1) * size].astype(out_ref.dtype)


def expand(place, refs, look_ref, row_ref):
    lane_group = iota((8, 128), 1) // SLOTS
    sample_iota = iota((BLOCK, 128), 0)
    meta_row = iota((META, 128), 0)
    for j, ref in enumerate(refs):
        looks, rows = [], []
        for m in range(NY):
            b = m * (BLOCK + META)
            meta = ref[b + BLOCK:b + BLOCK + META, :].astype(F32)
            high = jnp.sum(jnp.where(meta_row == place * 2, meta, 0.0), axis=0, keepdims=True).astype(I32)
            low = jnp.sum(jnp.where(meta_row == place * 2 + 1, meta, 0.0), axis=0, keepdims=True).astype(I32) + 256
            pick = (sample_iota == (low & 127)).astype(F32).astype(BF16)
            looks.append(dot(pick, ref[b:b + BLOCK, :], 0, 0).astype(BF16))
            rows.append(jnp.broadcast_to((high * 4 + (low >> 7)).astype(F32), (8, 128)))
        for d in range(NX):
            row = rows[d]
            for g in range(NX):
                m = (d - g) % NX
                look_ref[d, j, g * SLOTS:(g + 1) * SLOTS, :] = looks[m][g * SLOTS:(g + 1) * SLOTS]
                if g:
                    row = jnp.where(lane_group == g, rows[m], row)
            row_ref[d, j] = row


def scatter(d, looks, rows, out_ref, firsts=()):
    base = iota((512, 128), 0).astype(F32)
    look = jnp.concatenate([ref[d].reshape(-1, EMB) for ref in looks], axis=0)
    for i in range(ROWS // 512):
        here = base + float(i * 512)
        s = slice(i * 512, (i + 1) * 512)
        hot = jnp.concatenate([(here == ref[d, j, 0:1, :]).astype(BF16) for ref in rows for j in range(ref.shape[1])], axis=1)
        total = dot(hot, look, 1, 0)
        for first in firsts:
            total = total + first[s].astype(F32)
        out_ref[s] = total.astype(out_ref.dtype)


def expand_kernel(count, *refs):
    place = spot("zl") * 2 + spot("c")
    look_own, row_own, look_other, row_other = refs[count:]
    expand(place ^ 1, refs[:count], look_other, row_other)
    expand(place, refs[:count], look_own, row_own)


def scatter_kernel(ds, *refs):
    looks, rows, rest = refs[0:4:2], refs[1:4:2], refs[4:]
    count = len(ds)
    firsts, outs = rest[:-count], rest[-count:]
    for i, d in enumerate(ds):
        scatter(d, looks, rows, outs[i], firsts[i::count])


def update_kernel(a_ref, b_ref, c_ref, d_ref, table_ref, accum_ref, table_out, accum_out):
    eye = iota((128, 128), 0) == iota((128, 128), 1)
    for i in range(ROWS // 128):
        s = slice(i * 128, (i + 1) * 128)
        grad = a_ref[s].astype(F32) + b_ref[s].astype(F32)
        grad = grad + (c_ref[s].astype(F32) + d_ref[s].astype(F32))
        mean = jnp.sum(grad * grad, axis=1, keepdims=True) * (1.0 / EMB)
        old = jnp.sum(jnp.where(eye, accum_ref[i:i + 1, :], 0.0), axis=1, keepdims=True)
        new = old + mean
        table_out[s] = table_ref[s] - grad * (RATE / (jnp.sqrt(new) + EPSILON))
        accum_out[i:i + 1, :] = jnp.sum(jnp.where(eye, new, 0.0), axis=0, keepdims=True)


def ring(size, shift):
    return [(i, (i + shift) % size) for i in range(size)]


def shape(dims, kind):
    return jax.ShapeDtypeStruct(dims, kind)


def per_device(inputs, cotangent, cross_down, cross_up, cross_bias, indices, emb_table, row_accum):
    swap = ring(NC, 1)
    idx = jnp.transpose(indices, (1, 2, 0)).reshape(TABLES * HOT, BLOCK)

    def call(kernel, name, outs, operands, mib, work):
        return pl.pallas_call(
            kernel,
            out_shape=outs,
            in_specs=[VMEM] * len(operands),
            out_specs=(VMEM,) * len(outs) if isinstance(outs, tuple) else VMEM,
            compiler_params=params(mib),
            cost_estimate=work,
            name=name,
        )(*operands)

    meta = call(rank_kernel, "rank", shape((TABLES, META, 128), BF16), (idx,), 16, cost(2_000_000_000, 100_000))
    (inputs, cotangent, cross_down, cross_up), meta = lax.optimization_barrier(((inputs, cotangent, cross_down, cross_up), meta))
    pack, cols, both = call(
        hidden_kernel, "hidden",
        (shape((BLOCK, PACK), BF16), shape((BLOCK, RANK), BF16), shape((BLOCK, 2 * RANK), BF16)),
        (inputs, cotangent, cross_down, cross_up), 16, cost(500_000_000, 4_000_000),
    )
    dense_part, sent = call(
        pooled_kernel, "pooled",
        (shape((BLOCK, EMB), BF16), shape((NY, NZH, BLOCK + META, EMB), BF16)),
        (cotangent, both, cross_down, cross_up, cross_bias.reshape(FEATURES // 128, 128), meta),
        16, cost(300_000_000, 4_000_000),
    )

    other_pack = lax.ppermute(pack, "c", swap)
    along = [sent[0]] + [lax.ppermute(sent[d], "y", ring(NY, d)) for d in range(1, NY)]
    terms = call(
        weight_kernel, "weights", shape((NY, 128, FEATURES), BF16), (pack, cols, other_pack), 16, cost(300_000_000, 3_000_000)
    )
    along, _ = lax.optimization_barrier((along, terms))
    near = jnp.concatenate([v[0] for v in along], axis=0)
    far = jnp.concatenate([v[1] for v in along], axis=0)

    def cross(m):
        return lax.ppermute(far, ("zh", "zl"), [(i, (7 - i) ^ m) for i in range(8)])

    def line(m):
        return lax.ppermute(near, "zl", [(i, i ^ m) for i in range(NZL)])

    def pass_on(v):
        return lax.ppermute(v, "zl", [(i, i ^ 1) for i in range(NZL)])

    sent_on = [cross(2), cross(0), line(2)]
    blocks = [near] + sent_on + [line(1)]
    passed = [pass_on(v) for v in sent_on]

    def exchanged(v, axes):
        return lax.all_to_all(v, axes, split_axis=0, concat_axis=0, tiled=True)

    def added(v, dims, kind):
        return call(add_kernel, "add", shape(dims, kind), (v,), 16, cost(1_000, 1_000))

    def expanded(blocks):
        look = shape((NX, len(blocks), 128, EMB), BF16)
        row = shape((NX, len(blocks), 8, 128), F32)
        return call(
            functools.partial(expand_kernel, len(blocks)), "expand", (look, row, look, row), tuple(blocks), 16, cost(1_000, 1_000)
        )

    def scattered(arrays, ds, firsts=()):
        return call(
            functools.partial(scatter_kernel, ds), "scatter",
            (shape((ROWS, EMB), BF16),) * len(ds), (*arrays, *firsts), 24, cost(1_000, 1_000),
        )

    def swapped(vs):
        return [lax.ppermute(v, "c", swap) for v in vs]

    early = expanded(blocks)
    early, terms = lax.optimization_barrier((early, exchanged(terms, "y")))
    terms = added(terms, (32, 4, FEATURES), BF16)
    weight_total = added(exchanged(terms, ("zh", "zl", "x")), (4, FEATURES), F32)
    late, _ = lax.optimization_barrier((passed, terms))
    late = expanded(late)
    own, other = [*early[:2], *late[:2]], [*early[2:], *late[2:]]

    first = scattered(other, (2,))
    other, first = lax.optimization_barrier((other, first))
    (first,) = swapped(first)
    rest = scattered(other, (1, 3))
    own, rest = lax.optimization_barrier((own, rest))
    rest = swapped(rest)
    apart = scattered(own, (2,), (first,))
    own, apart = lax.optimization_barrier((own, apart))
    apart = lax.ppermute(apart[0], "x", ring(NX, 2))
    right, left = scattered(own, (1, 3), rest)
    other, right, left = lax.optimization_barrier((other, right, left))
    right = lax.ppermute(right, "x", ring(NX, 1))
    left = lax.ppermute(left, "x", ring(NX, 3))
    (here,) = scattered(own, (0,), swapped(scattered(other, (0,))))

    here, weight_total = lax.optimization_barrier((here, weight_total))

    table_new, accum_new = call(
        update_kernel, "update", (shape((ROWS, EMB), F32), shape((8, 128), F32)),
        (here, right, left, apart, emb_table, row_accum.reshape(8, 128)), 16, cost(1_000, 1_000),
    )
    return (table_new, accum_new.reshape(ROWS), dense_part, weight_total)


def solution(mesh):
    fine = Mesh(mesh.devices.reshape(NY, NZH, NX, NC, NZL), AXES)
    in_specs = (
        P(AXES, None), P(AXES, None), P(), P(), P(), P(AXES, None, None), P(AXES, None), P(AXES),
    )
    out_specs = (P(AXES, None), P(AXES), P(AXES, None), P(AXES, None))
    return jax.shard_map(per_device, mesh=fine, in_specs=in_specs, out_specs=out_specs, check_vma=False)
```

```python
import functools

import jax
import jax.numpy as jnp
from jax import lax
from jax.experimental import pallas as pl
from jax.experimental.pallas import tpu as pltpu
from jax.sharding import Mesh, PartitionSpec as P

EMB = 128
TABLES = 8
HOT = 8
RANK = 512
FEATURES = 1152
RATE = 0.1
EPSILON = 1e-08
BLOCK = 128
ROWS = 1024
SLOTS = 32
META = 16
AXES = ("y", "zh", "x", "c", "zl")
NY, NZH, NX, NC, NZL = 4, 2, 4, 2, 4
PACK = 2 * FEATURES + RANK
VMEM = pl.BlockSpec(memory_space=pltpu.VMEM)
BF16, F32, I32 = jnp.bfloat16, jnp.float32, jnp.int32


def dot(a, b, left, right):
    return lax.dot_general(a, b, (((left,), (right,)), ((), ())), preferred_element_type=F32)


def iota(shape, dim):
    return lax.broadcasted_iota(I32, shape, dim)


def params(mib):
    return pltpu.CompilerParams(vmem_limit_bytes=mib * 1024 * 1024)


def cost(flops, bytes_accessed):
    return pl.CostEstimate(flops=flops, bytes_accessed=bytes_accessed, transcendentals=0)


def spot(axis):
    return lax.axis_index(axis)


def rank_kernel(idx_ref, meta_ref):
    yy, xx = spot("y"), spot("x")
    upper = (iota((128, 128), 0) < iota((128, 128), 1)).astype(BF16)
    ones = jnp.ones((128, 128), BF16)
    sub32 = iota((32, 128), 0)
    sub128 = iota((128, 128), 0)
    pair = iota((META, 128), 0) // 2
    second = iota((META, 128), 0) % 2 == 1
    for t in range(TABLES):
        ahead = (t // 2 - yy) & 3
        idx = idx_ref[t * HOT:(t + 1) * HOT, :]
        owner = idx >> 10
        place = (owner & 3) * 2 + ((owner >> 2) & 1)
        group = ((owner >> 3) - xx - ahead) & 3
        full = place * 4 + group
        high = ((idx >> 2) & 255).astype(F32)
        low = ((idx & 3) * 128 + iota((HOT, 128), 1) - 256).astype(F32)
        hot = jnp.concatenate([(sub32 == full[k:k + 1]).astype(F32) for k in range(HOT)], axis=0)
        hot16 = hot.astype(BF16)
        before = dot(hot16, upper, 1, 0)
        total = dot(hot16, ones, 1, 0)
        base = jnp.zeros((32, 128), F32)
        slots, values = [], []
        for k in range(HOT):
            s = slice(k * 32, (k + 1) * 32)
            rank = jnp.sum(hot[s] * (before[s] + base), axis=0, keepdims=True).astype(I32)
            base = base + total[s]
            slots.append((sub128 == group[k:k + 1] * SLOTS + rank).astype(F32).astype(BF16))
            value = jnp.where(second, low[k:k + 1], high[k:k + 1])
            values.append(jnp.where(pair == place[k:k + 1], value, 0.0).astype(BF16))
        meta = dot(jnp.concatenate(values, axis=1), jnp.concatenate(slots, axis=1), 1, 1)
        meta_ref[t] = meta.astype(BF16)


def hidden_kernel(in_ref, cot_ref, down_ref, up_ref, pack_ref, cols_ref, both_ref):
    core = spot("c")
    inputs = in_ref[...]
    grad_scale = (cot_ref[...].astype(F32) * inputs.astype(F32)).astype(BF16)
    pack_ref[:, :FEATURES] = inputs
    pack_ref[:, FEATURES:2 * FEATURES] = grad_scale
    hidden = dot(inputs, down_ref[...], 1, 0).astype(BF16)
    grad_hidden = dot(grad_scale, up_ref[...], 1, 1).astype(BF16)
    both_ref[:, :RANK] = grad_hidden
    both_ref[:, RANK:] = hidden

    both = jnp.concatenate([grad_hidden, hidden], axis=1)
    src = iota((2 * RANK, RANK), 0)
    dst = iota((2 * RANK, RANK), 1)
    want = (dst >> 7) * 256 + ((dst >> 6) & 1) * 128 + ((dst >> 2) & 3) * 32 + ((dst >> 4) & 3) * 4 + (dst & 3)
    pack_ref[:, 2 * FEATURES:] = dot(both, (src == want + (1 - core) * 16).astype(F32).astype(BF16), 1, 0).astype(BF16)
    cols_ref[...] = dot(both, (src == want + core * 16).astype(F32).astype(BF16), 1, 0).astype(BF16)


def pooled_kernel(cot_ref, both_ref, down_ref, up_ref, bias_ref, meta_ref, dense_ref, sent_ref):
    yy, half = spot("y"), spot("zh")
    bias = jnp.concatenate([bias_ref[i:i + 1, :] for i in range(FEATURES // 128)], axis=1)
    scale = dot(both_ref[:, RANK:], up_ref[...], 1, 0) + bias
    back = dot(both_ref[:, :RANK], down_ref[...], 1, 1)
    grad = (cot_ref[...].astype(F32) * (scale + 1.0) + back).astype(BF16)
    dense_ref[...] = grad[:, :EMB]
    for t in range(TABLES):
        ahead, other = (t // 2 - yy) & 3, (t % 2) ^ half
        sent_ref[ahead, other, 0:BLOCK, :] = grad[:, (t + 1) * EMB:(t + 2) * EMB]
        sent_ref[ahead, other, BLOCK:BLOCK + META, :] = meta_ref[t]


def weight_kernel(pack_ref, cols_ref, other_ref, out_ref):
    for half in range(2):
        s = slice(half * 256, (half + 1) * 256)
        t = slice(half * FEATURES, (half + 1) * FEATURES)
        theirs = other_ref[:, 2 * FEATURES + half * 256:2 * FEATURES + (half + 1) * 256]
        left = jnp.concatenate([cols_ref[:, s], theirs], axis=0)
        right = jnp.concatenate([pack_ref[:, t], other_ref[:, t]], axis=0)
        out_ref[half * 2:half * 2 + 2] = dot(left, right, 0, 0).astype(BF16).reshape(2, 128, FEATURES)


def add_kernel(in_ref, out_ref):
    total = in_ref[0].astype(F32)
    for i in range(1, in_ref.shape[0]):
        total = total + in_ref[i].astype(F32)
    if len(out_ref.shape) == 2:
        out_ref[...] = total.astype(out_ref.dtype)
    else:
        size = out_ref.shape[1]
        for i in range(out_ref.shape[0]):
            out_ref[i] = total[i * size:(i + 1) * size].astype(out_ref.dtype)


def expand(place, refs, look_ref, row_ref):
    lane_group = iota((8, 128), 1) // SLOTS
    sample_iota = iota((BLOCK, 128), 0)
    meta_row = iota((META, 128), 0)
    for j, ref in enumerate(refs):
        looks, rows = [], []
        for m in range(NY):
            b = m * (BLOCK + META)
            meta = ref[b + BLOCK:b + BLOCK + META, :].astype(F32)
            high = jnp.sum(jnp.where(meta_row == place * 2, meta, 0.0), axis=0, keepdims=True).astype(I32)
            low = jnp.sum(jnp.where(meta_row == place * 2 + 1, meta, 0.0), axis=0, keepdims=True).astype(I32) + 256
            pick = (sample_iota == (low & 127)).astype(F32).astype(BF16)
            looks.append(dot(pick, ref[b:b + BLOCK, :], 0, 0).astype(BF16))
            rows.append(jnp.broadcast_to((high * 4 + (low >> 7)).astype(F32), (8, 128)))
        for d in range(NX):
            row = rows[d]
            for g in range(NX):
                m = (d - g) % NX
                look_ref[d, j, g * SLOTS:(g + 1) * SLOTS, :] = looks[m][g * SLOTS:(g + 1) * SLOTS]
                if g:
                    row = jnp.where(lane_group == g, rows[m], row)
            row_ref[d, j] = row


def scatter(d, looks, rows, out_ref, firsts=()):
    base = iota((1024, 128), 0).astype(F32)
    look = jnp.concatenate([ref[d].reshape(-1, EMB) for ref in looks], axis=0)
    for i in range(ROWS // 1024):
        here = base + float(i * 1024)
        s = slice(i * 1024, (i + 1) * 1024)
        hot = jnp.concatenate([(here == ref[d, j, 0:1, :]).astype(BF16) for ref in rows for j in range(ref.shape[1])], axis=1)
        total = dot(hot, look, 1, 0)
        for first in firsts:
            total = total + first[s].astype(F32)
        out_ref[s] = total.astype(out_ref.dtype)


def expand_kernel(count, *refs):
    place = spot("zl") * 2 + spot("c")
    look_own, row_own, look_other, row_other = refs[count:]
    expand(place ^ 1, refs[:count], look_other, row_other)
    expand(place, refs[:count], look_own, row_own)


def scatter_kernel(ds, *refs):
    looks, rows, rest = refs[0:4:2], refs[1:4:2], refs[4:]
    count = len(ds)
    firsts, outs = rest[:-count], rest[-count:]
    for i, d in enumerate(ds):
        scatter(d, looks, rows, outs[i], firsts[i::count])


def update_kernel(a_ref, b_ref, c_ref, d_ref, table_ref, accum_ref, table_out, accum_out):
    eye = iota((128, 128), 0) == iota((128, 128), 1)
    for i in range(ROWS // 128):
        s = slice(i * 128, (i + 1) * 128)
        grad = a_ref[s].astype(F32) + b_ref[s].astype(F32)
        grad = grad + (c_ref[s].astype(F32) + d_ref[s].astype(F32))
        mean = jnp.sum(grad * grad, axis=1, keepdims=True) * (1.0 / EMB)
        old = jnp.sum(jnp.where(eye, accum_ref[i:i + 1, :], 0.0), axis=1, keepdims=True)
        new = old + mean
        table_out[s] = table_ref[s] - grad * (RATE / (jnp.sqrt(new) + EPSILON))
        accum_out[i:i + 1, :] = jnp.sum(jnp.where(eye, new, 0.0), axis=0, keepdims=True)


def ring(size, shift):
    return [(i, (i + shift) % size) for i in range(size)]


def shape(dims, kind):
    return jax.ShapeDtypeStruct(dims, kind)


def per_device(inputs, cotangent, cross_down, cross_up, cross_bias, indices, emb_table, row_accum):
    swap = ring(NC, 1)
    idx = jnp.transpose(indices, (1, 2, 0)).reshape(TABLES * HOT, BLOCK)

    def call(kernel, name, outs, operands, mib, work):
        return pl.pallas_call(
            kernel,
            out_shape=outs,
            in_specs=[VMEM] * len(operands),
            out_specs=(VMEM,) * len(outs) if isinstance(outs, tuple) else VMEM,
            compiler_params=params(mib),
            cost_estimate=work,
            name=name,
        )(*operands)

    meta = call(rank_kernel, "rank", shape((TABLES, META, 128), BF16), (idx,), 16, cost(2_000_000_000, 100_000))
    (inputs, cotangent, cross_down, cross_up), meta = lax.optimization_barrier(((inputs, cotangent, cross_down, cross_up), meta))
    pack, cols, both = call(
        hidden_kernel, "hidden",
        (shape((BLOCK, PACK), BF16), shape((BLOCK, RANK), BF16), shape((BLOCK, 2 * RANK), BF16)),
        (inputs, cotangent, cross_down, cross_up), 16, cost(500_000_000, 4_000_000),
    )
    dense_part, sent = call(
        pooled_kernel, "pooled",
        (shape((BLOCK, EMB), BF16), shape((NY, NZH, BLOCK + META, EMB), BF16)),
        (cotangent, both, cross_down, cross_up, cross_bias.reshape(FEATURES // 128, 128), meta),
        16, cost(300_000_000, 4_000_000),
    )

    other_pack = lax.ppermute(pack, "c", swap)
    along = [sent[0]] + [lax.ppermute(sent[d], "y", ring(NY, d)) for d in range(1, NY)]
    terms = call(
        weight_kernel, "weights", shape((NY, 128, FEATURES), BF16), (pack, cols, other_pack), 16, cost(300_000_000, 3_000_000)
    )
    along, _ = lax.optimization_barrier((along, terms))
    near = jnp.concatenate([v[0] for v in along], axis=0)
    far = jnp.concatenate([v[1] for v in along], axis=0)

    def cross(m):
        return lax.ppermute(far, ("zh", "zl"), [(i, (7 - i) ^ m) for i in range(8)])

    def line(m):
        return lax.ppermute(near, "zl", [(i, i ^ m) for i in range(NZL)])

    def pass_on(v):
        return lax.ppermute(v, "zl", [(i, i ^ 1) for i in range(NZL)])

    sent_on = [cross(2), cross(0), line(2)]
    blocks = [near] + sent_on + [line(1)]
    passed = [pass_on(v) for v in sent_on]

    def exchanged(v, axes):
        return lax.all_to_all(v, axes, split_axis=0, concat_axis=0, tiled=True)

    def added(v, dims, kind):
        return call(add_kernel, "add", shape(dims, kind), (v,), 16, cost(1_000, 1_000))

    def expanded(blocks):
        look = shape((NX, len(blocks), 128, EMB), BF16)
        row = shape((NX, len(blocks), 8, 128), F32)
        return call(
            functools.partial(expand_kernel, len(blocks)), "expand", (look, row, look, row), tuple(blocks), 16, cost(1_000, 1_000)
        )

    def scattered(arrays, ds, firsts=()):
        return call(
            functools.partial(scatter_kernel, ds), "scatter",
            (shape((ROWS, EMB), BF16),) * len(ds), (*arrays, *firsts), 24, cost(1_000, 1_000),
        )

    def swapped(vs):
        return [lax.ppermute(v, "c", swap) for v in vs]

    early = expanded(blocks)
    early, terms = lax.optimization_barrier((early, exchanged(terms, "y")))
    terms = added(terms, (32, 4, FEATURES), BF16)
    weight_total = added(exchanged(terms, ("zh", "zl", "x")), (4, FEATURES), F32)
    late, _ = lax.optimization_barrier((passed, terms))
    late = expanded(late)
    own, other = [*early[:2], *late[:2]], [*early[2:], *late[2:]]

    first = scattered(other, (2,))
    other, first = lax.optimization_barrier((other, first))
    (first,) = swapped(first)
    rest = scattered(other, (1, 3))
    own, rest = lax.optimization_barrier((own, rest))
    rest = swapped(rest)
    apart = scattered(own, (2,), (first,))
    own, apart = lax.optimization_barrier((own, apart))
    apart = lax.ppermute(apart[0], "x", ring(NX, 2))
    right, left = scattered(own, (1, 3), rest)
    other, right, left = lax.optimization_barrier((other, right, left))
    right = lax.ppermute(right, "x", ring(NX, 1))
    left = lax.ppermute(left, "x", ring(NX, 3))
    (here,) = scattered(own, (0,), swapped(scattered(other, (0,))))

    here, weight_total = lax.optimization_barrier((here, weight_total))

    table_new, accum_new = call(
        update_kernel, "update", (shape((ROWS, EMB), F32), shape((8, 128), F32)),
        (here, right, left, apart, emb_table, row_accum.reshape(8, 128)), 16, cost(1_000, 1_000),
    )
    return (table_new, accum_new.reshape(ROWS), dense_part, weight_total)


def solution(mesh):
    fine = Mesh(mesh.devices.reshape(NY, NZH, NX, NC, NZL), AXES)
    in_specs = (
        P(AXES, None), P(AXES, None), P(), P(), P(), P(AXES, None, None), P(AXES, None), P(AXES),
    )
    out_specs = (P(AXES, None), P(AXES), P(AXES, None), P(AXES, None))
    return jax.shard_map(per_device, mesh=fine, in_specs=in_specs, out_specs=out_specs, check_vma=False)
```
